256 devices in a mesh: region: 64 (over z, x, core), sub: 4 (over y).
Axes of the slice: x: 4, y: 4, z: 8, core: 2. Of those that a mesh axis runs over, the one named last changes fastest.
Arguments:
- points: float32 [3, 1024, 512], P(None, 'region'), may hold values from 0 to 64, as said below
- noise_var: float32 [1024, 512], P('region'), may hold values from 0.5 to 4
- right_sides: float32 [1024, 16, 512], P('region'), may hold values from -14 to 14
- pair_list: int32 [64, 4, 2, 80], P('region', 'sub'), may hold values from 0 to 31, as said below
- pair_count: int32 [64, 4], P('region', 'sub'), may hold values from 0 to 80, as said below
Outputs:
- solution: float32 [1024, 16, 512], P(('region', 'sub'))
The draws below stay inside these ranges and needn't reach their ends.
Inputs may be any that keep to these rules, and one draw needn't show every extreme that they name: `points`: block b is a unit cell of a grid of 64 x 4 x 4 cells: region r holds layer r along the first coordinate, its 16 blocks each layer in Morton order of the other two cell indices; every point of a block lies in its cell. `pair_list`: in each device's slots below its pair_count stand pairs (i, j): i a block of the device's region counted from 0, j a block of the region or 16 plus a block of the next region's first layer. Over the devices of a region, every unordered pair of a block of the region and a block of the region or the next region whose cells differ by at most one in every index is listed exactly once, with its first entry in the region. Other slots hold 0. `pair_count`: in every region but the last one device lists exactly 80 pairs.
All inputs are finite; a program needn't handle non-finite values.
Results may differ from the reference program's by a relative error of at most 0.00036.
Values may be sent and summed in bfloat16 or wider, within the bound.
No kernel may reach another device: no remote copies, remote signals or barrier semaphores. Data moves between devices by JAX's collectives and lax.ppermute only.
A program may use at most 64 MiB of HBM per device.

```python
import math
import jax
import jax.numpy as jnp
from jax import lax

BLOCK = 512
RHS = 16
SIDE = 4
DEPTH = 1
ITERS = 2
LAYER = 16
BLK_REG = 16
PAIRS = 80
REGIONS = 64
SUBS = 4
NBLK = 1024


def cell_of(block_index):
    depth_now = block_index // LAYER
    inner = block_index % LAYER
    grid_row = jnp.zeros_like(inner)
    grid_col = jnp.zeros_like(inner)
    for bit_place in range(SIDE.bit_length() - 1):
        grid_row = grid_row + inner // 4 ** bit_place % 2 * 2 ** bit_place
        grid_col = grid_col + inner // (2 * 4 ** bit_place) % 2 * 2 ** bit_place
    return (depth_now, grid_row, grid_col)


def morton_code(grid_row, grid_col):
    code_total = jnp.zeros_like(grid_row)
    for bit_place in range(SIDE.bit_length() - 1):
        code_total = code_total + grid_row // 2 ** bit_place % 2 * 4 ** bit_place
        code_total = code_total + grid_col // 2 ** bit_place % 2 * (2 * 4 ** bit_place)
    return code_total


def region_pairs(key):
    pair_key = jax.random.fold_in(key, 50)
    blocks_here = jnp.arange(BLK_REG, dtype=jnp.int32)
    depth_now, grid_row, grid_col = cell_of(blocks_here)
    forward = [(0, 0, 0), (0, 0, 1), (0, 1, -1), (0, 1, 0), (0, 1, 1)]
    forward = forward + [(1, step_a, step_b) for step_a in (-1, 0, 1) for step_b in (-1, 0, 1)]
    candidates = len(forward) * BLK_REG
    ranks = jnp.arange(candidates, dtype=jnp.int32)

    def one_region(region):
        region_key = jax.random.fold_in(pair_key, region)
        valid_parts = []
        first_parts = []
        second_parts = []
        for step_x, step_y, step_z in forward:
            new_row = grid_row + step_y
            new_col = grid_col + step_z
            new_depth = depth_now + step_x
            inside = (new_row >= 0) & (new_row < SIDE) & (new_col >= 0) & (new_col < SIDE)
            inside = inside & (region * DEPTH + new_depth < REGIONS * DEPTH)
            code_here = morton_code(jnp.clip(new_row, 0, SIDE - 1), jnp.clip(new_col, 0, SIDE - 1))
            target = jnp.where(new_depth < DEPTH, new_depth * LAYER + code_here, BLK_REG + code_here)
            valid_parts.append(inside.astype(jnp.int32))
            first_parts.append(blocks_here)
            second_parts.append(target.astype(jnp.int32))
        valid = jnp.concatenate(valid_parts)
        first_rows = jnp.concatenate(first_parts)
        second_rows = jnp.concatenate(second_parts)
        shuffle = jax.random.permutation(region_key, candidates).astype(jnp.int32)
        order = jnp.argsort(-(valid * candidates + shuffle), stable=True)
        live_total = jnp.sum(valid)
        heavy = jax.random.randint(jax.random.fold_in(region_key, 1), (), 0, SUBS, dtype=jnp.int32)
        spare = (ranks - PAIRS) % (SUBS - 1)
        device = jnp.where(ranks < PAIRS, heavy, spare + (spare >= heavy).astype(jnp.int32))
        place = jnp.where(ranks < PAIRS, ranks, (ranks - PAIRS) // (SUBS - 1))
        alive = ranks < live_total
        target_slot = jnp.where(alive, device * PAIRS + place, SUBS * PAIRS)
        firsts = jnp.zeros((SUBS * PAIRS + 1,), jnp.int32).at[target_slot].set(first_rows[order])
        seconds = jnp.zeros((SUBS * PAIRS + 1,), jnp.int32).at[target_slot].set(second_rows[order])
        counts = jnp.zeros((SUBS,), jnp.int32).at[device].add(alive.astype(jnp.int32))
        listing = jnp.stack([firsts[:-1].reshape(SUBS, PAIRS), seconds[:-1].reshape(SUBS, PAIRS)], axis=1)
        return (listing, counts)
    return jax.vmap(one_region)(jnp.arange(REGIONS, dtype=jnp.int32))


def draw_pair_list(key, part):
    return region_pairs(key)[0]


def draw_pair_count(key, part):
    return region_pairs(key)[1]


def draw_points(key, part):
    key = jax.random.fold_in(key, 1)
    jitter = jax.random.uniform(key, (3, NBLK, BLOCK), jnp.float32)
    everything = jnp.arange(NBLK, dtype=jnp.int32)
    depth_now, grid_row, grid_col = cell_of(everything % BLK_REG)
    first_cell = everything // BLK_REG * DEPTH + depth_now
    first_axis = first_cell.astype(jnp.float32)[:, None] + jitter[0]
    second_axis = grid_row.astype(jnp.float32)[:, None] + jitter[1]
    third_axis = grid_col.astype(jnp.float32)[:, None] + jitter[2]
    return jnp.stack([first_axis, second_axis, third_axis])


def draw_right_sides(key, part):
    key = jax.random.fold_in(key, 2)
    rising = 1.0 + 2.0 * jnp.arange(NBLK, dtype=jnp.int32).astype(jnp.float32) / max(NBLK - 1, 1)
    values = jax.random.truncated_normal(key, -4.0, 4.0, (NBLK, RHS, BLOCK), jnp.float32)
    return values * rising[:, None, None]


def level_of(rng, shape, cuts, low, top_value):
    level, own = 1.0, jax.random.fold_in(rng, 6)
    for axis_at, blocks in cuts:
        steps = jnp.exp(jax.random.uniform(jax.random.fold_in(own, axis_at), (blocks,), jnp.float32, low / len(cuts), top_value / len(cuts)))
        level = level * jnp.repeat(steps, shape[axis_at] // blocks).reshape([-1 if axis == axis_at else 1 for axis in range(len(shape))])
    return level


def setup_inputs(seed: int = 0) -> dict:
    arg_keys = jax.random.split(jax.random.key(seed), 6)
    points = draw_points(jax.random.fold_in(arg_keys[5], 71), 0)
    noise_var = jnp.clip(jnp.exp(math.log(4.0) - 2.0794415 * jax.random.uniform(arg_keys[1], (NBLK, BLOCK), jnp.float32) ** level_of(arg_keys[1], (NBLK, BLOCK), ((0, 64),), -0.2, 0.2)), 0.5, 4.0)
    right_sides = draw_right_sides(jax.random.fold_in(arg_keys[5], 71), 0)
    pair_list = draw_pair_list(jax.random.fold_in(arg_keys[5], 71), 0)
    pair_count = draw_pair_count(jax.random.fold_in(arg_keys[5], 71), 0)
    return {"points": points, "noise_var": noise_var, "right_sides": right_sides, "pair_list": pair_list, "pair_count": pair_count}


support_radius = 1.0

def kernel_tile(left_points, right_points):
    squared = jnp.zeros((left_points.shape[0], left_points.shape[2], right_points.shape[2]), jnp.float32)
    for component in range(3):
        spread = left_points[:, component, :, None] - right_points[:, component, None, :]
        squared = squared + spread * spread
    radius = jnp.sqrt(squared) / support_radius
    falloff = jnp.maximum(1.0 - radius, 0.0)
    return (falloff ** 4 * (4.0 * radius + 1.0)).astype(jnp.bfloat16)

def inner_products(left_field, right_field):
    return jnp.einsum('brp,bsp->rs', left_field, right_field, precision=lax.Precision.HIGHEST)

def combine_columns(matrix, vectors):
    return jnp.einsum('rs,brp->bsp', matrix, vectors, precision=lax.Precision.HIGHEST)

def spd_solve(matrix, right_part):
    lower = jnp.linalg.cholesky(matrix)
    middle = lax.linalg.triangular_solve(lower, right_part, left_side=True, lower=True)
    return lax.linalg.triangular_solve(lower, middle, left_side=True, lower=True, transpose_a=True)

def reference(points, noise_var, right_sides, pair_list, pair_count):
    block_points = jnp.transpose(points, (1, 0, 2))
    offsets = (jnp.arange(REGIONS, dtype=jnp.int32) * BLK_REG)[:, None, None]
    rows_left = (pair_list[:, :, 0, :] + offsets).reshape(-1).astype(jnp.int32)
    rows_right = (pair_list[:, :, 1, :] + offsets).reshape(-1).astype(jnp.int32)
    alive = (jnp.arange(PAIRS, dtype=jnp.int32)[None, None, :] < pair_count[:, :, None]).reshape(-1)
    group_size = 32
    padding = -rows_left.shape[0] % group_size
    rows_left = jnp.pad(rows_left, (0, padding)).reshape(-1, group_size)
    rows_right = jnp.pad(rows_right, (0, padding)).reshape(-1, group_size)
    alive = jnp.pad(alive, (0, padding)).reshape(-1, group_size)

    def apply_operator(directions):
        rounded = directions.astype(jnp.bfloat16)

        def one_group(totals, item):
            left_rows, right_rows, alive_rows = item
            tiles = kernel_tile(block_points[left_rows], block_points[right_rows]).astype(jnp.float32)
            to_left = jnp.einsum('grb,gab->gra', rounded[right_rows].astype(jnp.float32), tiles, precision=lax.Precision.HIGHEST)
            to_right = jnp.einsum('gra,gab->grb', rounded[left_rows].astype(jnp.float32), tiles, precision=lax.Precision.HIGHEST)
            weight_left = alive_rows.astype(jnp.float32)[:, None, None]
            weight_right = (alive_rows & (left_rows != right_rows)).astype(jnp.float32)[:, None, None]
            totals = totals.at[left_rows].add(to_left * weight_left)
            totals = totals.at[right_rows].add(to_right * weight_right)
            return (totals, None)
        totals, unused = lax.scan(one_group, jnp.zeros(directions.shape, jnp.float32), (rows_left, rows_right, alive))
        return totals + noise_var[:, None, :] * directions
    solution = jnp.zeros(right_sides.shape, jnp.float32)
    residual = right_sides
    directions = right_sides
    current = inner_products(residual, residual)
    for sweep in range(ITERS):
        image = apply_operator(directions)
        step_size = spd_solve(inner_products(directions, image), current)
        solution = solution + combine_columns(step_size, directions)
        residual = residual - combine_columns(step_size, image)
        if sweep + 1 < ITERS:
            following = inner_products(residual, residual)
            momentum = spd_solve(current, following)
            directions = residual + combine_columns(momentum, directions)
            current = following
    return solution
```

```python
import functools
import jax
import jax.numpy as jnp
from jax import lax
from jax.experimental import pallas as pl
from jax.experimental.pallas import tpu as pltpu
from jax.sharding import PartitionSpec as P

OWN = ((0, 0), (0, 1), (1, 0), (1, 1))
BORDER = ((0, 2), (1, 2), (2, 0), (2, 1), (2, 2))
WINDOW = OWN + BORDER
PAIRED = tuple((i, j) for j in range(4) for i in range(j))
CROSS = tuple(
    (i, j)
    for j in range(4, 9)
    for i in range(4)
    if max(abs(OWN[i][0] - WINDOW[j][0]), abs(OWN[i][1] - WINDOW[j][1])) <= 1
)
BLOCK = 512
RHS = 16
FEATURES = 64
f32, bf16 = jnp.float32, jnp.bfloat16
VMEM = pl.BlockSpec(memory_space=pltpu.VMEM)


def lookup(values, step):
    result = jnp.int32(0)
    for start in range(0, len(values), 8):
        code = 0
        for place, value in enumerate(values[start:start + 8]):
            code |= value << (4 * place)
        if code >= 1 << 31:
            code -= 1 << 32
        part = lax.shift_right_logical(jnp.int32(code), 4 * (step - start)) & 15
        result = part if start == 0 else jnp.where(step >= start, part, result)
    return result


def call(kernel, name, out_shape, args, flops, aliases=None):
    return pl.pallas_call(
        kernel,
        name=name,
        out_shape=out_shape,
        in_specs=[VMEM] * len(args),
        out_specs=jax.tree.map(lambda _: VMEM, out_shape),
        input_output_aliases=aliases or {},
        compiler_params=pltpu.CompilerParams(vmem_limit_bytes=16 << 20),
        cost_estimate=pl.CostEstimate(flops=flops, bytes_accessed=1 << 20, transcendentals=0),
    )(*args)


def split(value):
    high = value.astype(bf16).astype(f32)
    rest = value - high
    middle = rest.astype(bf16).astype(f32)
    return high, middle, rest - middle


def feature_rows(place):
    rows = lax.broadcasted_iota(jnp.int32, place.shape, 0)
    parts = split(place)
    norms = split(16.0 * jnp.sum(place * place, axis=0, keepdims=True))
    left, right = [], []
    for group, (a, b) in enumerate(((0, 0), (0, 1), (1, 0), (1, 1), (0, 2), (2, 0), (1, 2), (2, 1))):
        one_left, one_right = -32.0 * parts[a], parts[b]
        if group < 3:
            norm = jnp.broadcast_to(norms[group], place.shape)
            one_left = jnp.where(rows == 3, norm, jnp.where(rows == 4, 1.0, one_left))
            one_right = jnp.where(rows == 4, norm, jnp.where(rows == 3, 1.0, one_right))
        left.append(one_left)
        right.append(one_right)
    return jnp.concatenate(left, axis=0), jnp.concatenate(right, axis=0)


def prepare(points, noise_var, right_sides, sent, left, right, own_sides, own_noise):
    region = lax.axis_index("region")
    member = lax.axis_index("sub")
    row_half, column_half = member & 1, member >> 1
    rows = lax.broadcasted_iota(jnp.int32, (8, BLOCK), 0)
    centers = (
        region.astype(f32) + 0.5,
        row_half.astype(f32) + 1.5,
        column_half.astype(f32) + 1.5,
    )
    for index, (row, column) in enumerate(WINDOW):
        row = jnp.where(row_half == 1, 3 - row, row)
        column = jnp.where(column_half == 1, 3 - column, column)
        block = (row & 1) + 2 * (column & 1) + 4 * (row >> 1) + 8 * (column >> 1)
        place = jnp.zeros((8, BLOCK), f32)
        for axis in range(3):
            line = points[axis, pl.ds(block, 1), :] - centers[axis]
            place = jnp.where(rows == axis, jnp.broadcast_to(line, place.shape), place)
        side = right_sides[block]
        sent[index, 0:16, :] = side.astype(bf16)
        high, middle, low = split(place)
        sent[index, 16:32, :] = jnp.concatenate(
            [high + pltpu.roll(low, 3, 0), middle], axis=0
        ).astype(bf16)
        left_rows, right_rows = feature_rows(place)
        left[index] = jnp.transpose(left_rows).astype(bf16)
        if index < 4:
            right[index] = right_rows.astype(bf16)
            own_sides[index] = side
            own_noise[index] = noise_var[pl.ds(block, 1), :]


def neighbour_left(packed, shift):
    rows = lax.broadcasted_iota(jnp.int32, (8, BLOCK), 0)
    packed = packed.astype(f32)
    top, middle = packed[0:8], packed[8:16]
    place = jnp.where(rows < 3, top + middle + pltpu.roll(top, 5, 0), 0.0)
    place = jnp.where(rows == 0, place + shift, place)
    return jnp.transpose(feature_rows(place)[0]).astype(bf16)


def tile_of(left, right):
    squared = jnp.dot(left, right, preferred_element_type=f32)
    squared = jnp.maximum(squared, 1e-30)
    falloff = jnp.maximum(4.0 - squared * lax.rsqrt(squared), 0.0)
    second = falloff * falloff
    return ((second * second) * (5.0 - falloff)).astype(bf16)


def times(vectors, tile):
    return jnp.dot(vectors, tile, preferred_element_type=f32)


def times_transposed(vectors, tile):
    return lax.dot_general(vectors, tile, (((1,), (1,)), ((), ())), preferred_element_type=f32)


def within_layer(sent, left, right, totals, tiles):
    totals[...] = jnp.zeros_like(totals)

    def one_self(step, carry):
        tile = tile_of(left[step], right[step])
        tiles[step] = tile
        totals[step] += times(sent[step, 0:16, :], tile)
        return carry

    def one_pair(step, carry):
        i = lookup([p[0] for p in PAIRED], step)
        j = lookup([p[1] for p in PAIRED], step)
        tile = tile_of(left[j], right[i])
        tiles[4 + step] = tile
        totals[i] += times(sent[j, 0:16, :], tile)
        totals[j] += times_transposed(sent[i, 0:16, :], tile)
        return carry

    def one_cross(step, carry):
        i = lookup([p[0] for p in CROSS], step)
        j = lookup([p[1] for p in CROSS], step)
        tile = tile_of(left[j], right[i])
        tiles[10 + step] = tile
        totals[i] += times(sent[j, 0:16, :], tile)
        return carry

    lax.fori_loop(0, 4, one_self, 0, unroll=4)
    lax.fori_loop(0, 6, one_pair, 0, unroll=3)
    lax.fori_loop(0, 9, one_cross, 0, unroll=3)


def above_own(sent, right, above, before, totals, passed, tiles):
    totals[...] = before[...]
    passed[...] = jnp.zeros_like(passed)

    def one_block(j, carry):
        left = neighbour_left(above[j, 16:32, :], 1.0)
        for i in range(4):
            tile = tile_of(left, right[i])
            tiles[4 * j + i] = tile
            totals[i] += times(above[j, 0:16, :], tile)
            passed[j] += times_transposed(sent[i, 0:16, :], tile)
        return carry

    lax.fori_loop(0, 4, one_block, 0)


def across(right, above, below, before, totals, tiles, left_above, left_below):
    totals[...] = before[...]
    for j in range(5):
        left_above[j] = neighbour_left(above[4 + j, 16:32, :], 1.0)
        left_below[j] = neighbour_left(below[j, 16:32, :], -1.0)

    def one_above(step, carry):
        i = lookup([p[0] for p in CROSS], step)
        j = lookup([p[1] for p in CROSS], step)
        tile = tile_of(left_above[j - 4], right[i])
        tiles[step] = tile
        totals[i] += times(above[j, 0:16, :], tile)
        tile = tile_of(left_below[j - 4], right[i])
        totals[i] += times(below[j - 4, 0:16, :], tile)
        return carry

    lax.fori_loop(0, 9, one_above, 0, unroll=3)


def finish_image(totals, arrived, own_noise, own_sides, image, rounded):
    value = (totals[...] + arrived[...]) * (1.0 / 256.0) + own_noise[...] * own_sides[...]
    image[...] = value
    rounded[...] = value.astype(bf16)


def gram(first, second):
    return lax.dot_general(
        first, second, (((1,), (1,)), ((), ())),
        precision=lax.Precision.HIGHEST, preferred_element_type=f32,
    )


def inside(own_sides, image, rounded, own_noise, tiles, products, partial):
    total = jnp.zeros((32, 32), f32)
    for i in range(4):
        both = jnp.concatenate([image[i], own_sides[i]], axis=0)
        total += gram(both, both)
    products[...] = total
    partial[...] = own_noise[...] * image[...] * 256.0

    def one_self(step, carry):
        partial[step] += times(rounded[step], tiles[step])
        return carry

    def one_pair(step, carry):
        i = lookup([p[0] for p in PAIRED], step)
        j = lookup([p[1] for p in PAIRED], step)
        partial[i] += 2.0 * times(rounded[j], tiles[4 + step])
        return carry

    lax.fori_loop(0, 4, one_self, 0, unroll=4)
    lax.fori_loop(0, 6, one_pair, 0, unroll=6)


def upward(above, tiles, before, partial):
    partial[...] = before[...]

    def one_block(i, carry):
        total = jnp.zeros((RHS, BLOCK), f32)
        for j in range(4):
            total += times(above[j], tiles[4 * j + i])
        partial[i] += 2.0 * total
        return carry

    lax.fori_loop(0, 4, one_block, 0, unroll=2)


def sideways(from_row, from_column, from_corner, tiles_here, tiles_above, before, image, products, system):
    partial = [before[i] for i in range(4)]
    sources = {4: (from_column, 0), 5: (from_column, 1), 6: (from_row, 0), 7: (from_row, 1), 8: (from_corner, 0)}
    for step, (i, j) in enumerate(CROSS):
        ref, place = sources[j]
        partial[i] += times(ref[0, place], tiles_here[10 + step])
        partial[i] += 2.0 * times(ref[1, place], tiles_above[step])
    third = jnp.zeros((RHS, RHS), f32)
    for i in range(4):
        third += gram(image[i], partial[i])
    known = products[...]
    second, mixed = known[0:16, 0:16], known[0:16, 16:32]
    crossed, start = known[16:32, 0:16], known[16:32, 16:32]
    third = third * (1.0 / 256.0)
    top = jnp.concatenate([crossed, second, start, jnp.zeros((RHS, 80), f32)], axis=1)
    bottom = jnp.concatenate([second, third, mixed, jnp.zeros((RHS, 80), f32)], axis=1)
    system[...] = jnp.concatenate([top, bottom], axis=0)


def conclude(system, own_sides, image, result):
    value = system[...]
    lanes = lax.broadcasted_iota(jnp.int32, (32, 128), 1)
    rows = lax.broadcasted_iota(jnp.int32, (32, 128), 0)
    flipped = jnp.transpose(jnp.concatenate([value, jnp.zeros((96, 128), f32)], axis=0))[0:32]
    value = jnp.where(lanes < 32, 0.5 * (value + flipped), value)
    for k in range(32):
        pivot = value[k:k + 1, :]
        scaled = pivot * (1.0 / pivot[:, k:k + 1])
        value = jnp.where(rows == k, scaled, value - value[:, k:k + 1] * scaled)
    weights = jnp.transpose(jnp.concatenate([value, jnp.zeros((96, 128), f32)], axis=0))[32:48, 0:32]
    member = lax.axis_index("sub")
    for i, (row, column) in enumerate(OWN):
        both = jnp.concatenate([own_sides[i], image[i]], axis=0)
        place = (row ^ (member & 1)) + 2 * (column ^ (member >> 1))
        result[place] = jnp.dot(
            weights, both, precision=lax.Precision.HIGHEST, preferred_element_type=f32
        )


def local(regions, members, points, noise_var, right_sides, pair_list, pair_count):
    everyone = regions * members

    def from_region(value, step):
        pairs = [
            (source, source - step)
            for source in range(regions)
            if 0 <= source - step < regions
        ]
        return lax.ppermute(value, "region", pairs)

    def from_member(value, mask):
        return lax.ppermute(value, "sub", [(source, source ^ mask) for source in range(members)])

    def sum_over_all(value):
        low = 1
        while low < everyone:
            value = value + sum(
                lax.ppermute(
                    value,
                    ("region", "sub"),
                    [(source, source ^ (low * mask)) for source in range(everyone)],
                )
                for mask in (1, 2, 3)
            )
            low *= 4
        return value

    def shape(*dims, dtype=f32):
        return jax.ShapeDtypeStruct(dims, dtype)

    def held(*dims, dtype=bf16):
        return pltpu.VMEM(dims, dtype)

    tile_flops = 2 * BLOCK * BLOCK * 256
    field = (4, RHS, BLOCK)
    sent, left, right, own_sides, own_noise = call(
        prepare, "prepare",
        (shape(9, 32, BLOCK, dtype=bf16), shape(9, BLOCK, FEATURES, dtype=bf16),
         shape(4, FEATURES, BLOCK, dtype=bf16), shape(*field), shape(4, 1, BLOCK)),
        (points, noise_var, right_sides), tile_flops,
    )
    above = from_region(sent, 1)
    below = from_region(sent[4:9], -1)
    totals, tiles_here = call(
        within_layer, "within_layer", (shape(*field), held(19, BLOCK, BLOCK)),
        (sent, left, right), 19 * 4 * tile_flops,
    )
    totals, passed, tiles_up = call(
        above_own, "above_own", (shape(*field), shape(*field), held(16, BLOCK, BLOCK)),
        (sent, right, above, totals), 16 * 4 * tile_flops,
    )
    arrived = from_region(passed, -1)
    totals, tiles_side = pl.pallas_call(
        across, name="across",
        out_shape=(shape(*field), held(9, BLOCK, BLOCK)),
        in_specs=[VMEM] * 4, out_specs=(VMEM, VMEM),
        scratch_shapes=[pltpu.VMEM((5, BLOCK, FEATURES), bf16)] * 2,
        compiler_params=pltpu.CompilerParams(vmem_limit_bytes=16 << 20),
        cost_estimate=pl.CostEstimate(flops=18 * 4 * tile_flops, bytes_accessed=1 << 20, transcendentals=0),
    )(right, above, below, totals)
    image, rounded = call(
        finish_image, "finish_image", (shape(*field), shape(*field, dtype=bf16)),
        (totals, arrived, own_noise, own_sides), tile_flops // 8,
    )
    upper = from_region(rounded, 1)
    products, partial = call(
        inside, "inside", (shape(32, 32), shape(*field)),
        (own_sides, image, rounded, own_noise, tiles_here), 10 * 2 * tile_flops,
    )
    layers = jnp.stack([rounded, upper])
    from_row = from_member(layers[:, 2:4], 1)
    from_column = from_member(layers[:, 1::2], 2)
    from_corner = from_member(layers[:, 3:4], 3)
    partial = call(
        upward, "upward", shape(*field), (upper, tiles_up, partial), 16 * 2 * tile_flops,
    )
    system = call(
        sideways, "sideways", shape(32, 128),
        (from_row, from_column, from_corner, tiles_here, tiles_side, partial, image, products),
        18 * 2 * tile_flops,
    )
    system = sum_over_all(system)
    return call(
        conclude, "conclude", shape(*field), (system, own_sides, image), tile_flops,
    )


def solution(mesh):
    return jax.shard_map(
        functools.partial(local, mesh.shape["region"], mesh.shape["sub"]),
        mesh=mesh,
        in_specs=(
            P(None, "region", None),
            P("region", None),
            P("region", None, None),
            P("region", "sub", None, None),
            P("region", "sub"),
        ),
        out_specs=P(("region", "sub"), None, None),
        check_vma=False,
    )
```

```python
import functools
import jax
import jax.numpy as jnp
from jax import lax
from jax.experimental import pallas as pl
from jax.experimental.pallas import tpu as pltpu
from jax.sharding import PartitionSpec as P

OWN = ((0, 0), (0, 1), (1, 0), (1, 1))
BORDER = ((0, 2), (1, 2), (2, 0), (2, 1), (2, 2))
WINDOW = OWN + BORDER
PAIRED = tuple((i, j) for j in range(4) for i in range(j))
SELF = tuple((i, i) for i in range(4))
CROSS = tuple(
    (i, j)
    for j in range(4, 9)
    for i in range(4)
    if max(abs(OWN[i][0] - WINDOW[j][0]), abs(OWN[i][1] - WINDOW[j][1])) <= 1
)
BLOCK = 512
RHS = 16
FEATURES = 64
f32, bf16 = jnp.float32, jnp.bfloat16
VMEM = pl.BlockSpec(memory_space=pltpu.VMEM)


def call(kernel, name, out_shape, args, flops, scratch=(), args_space=pltpu.VMEM):
    return pl.pallas_call(
        kernel,
        name=name,
        out_shape=out_shape,
        in_specs=[pl.BlockSpec(memory_space=args_space)] * len(args),
        out_specs=jax.tree.map(lambda _: VMEM, out_shape),
        scratch_shapes=scratch,
        compiler_params=pltpu.CompilerParams(vmem_limit_bytes=16 << 20),
        cost_estimate=pl.CostEstimate(flops=flops, bytes_accessed=1 << 20, transcendentals=0),
    )(*args)


def split(value):
    high = value.astype(bf16).astype(f32)
    rest = value - high
    middle = rest.astype(bf16).astype(f32)
    return high, middle, rest - middle


def feature_rows(place):
    rows = lax.broadcasted_iota(jnp.int32, place.shape, 0)
    parts = split(place)
    norms = split(16.0 * jnp.sum(place * place, axis=0, keepdims=True))
    left, right = [], []
    for group, (a, b) in enumerate(((0, 0), (0, 1), (1, 0), (1, 1), (0, 2), (2, 0), (1, 2), (2, 1))):
        one_left, one_right = -32.0 * parts[a], parts[b]
        if group < 3:
            norm = jnp.broadcast_to(norms[group], place.shape)
            one_left = jnp.where(rows == 3, norm, jnp.where(rows == 4, 1.0, one_left))
            one_right = jnp.where(rows == 4, norm, jnp.where(rows == 3, 1.0, one_right))
        left.append(one_left)
        right.append(one_right)
    return jnp.concatenate(left, axis=0), jnp.concatenate(right, axis=0)


def prepare(
    points_far, noise_far, sides_far, sent, left, right, own_sides, own_noise,
    points, noise_var, right_sides, arrivals,
):
    copies = [
        pltpu.make_async_copy(source, target, arrivals.at[place])
        for place, (source, target) in enumerate(
            ((points_far, points), (noise_far, noise_var), (sides_far, right_sides))
        )
    ]
    for copy in copies:
        copy.start()
    for copy in copies:
        copy.wait()
    region = lax.axis_index("region")
    member = lax.axis_index("sub")
    row_half, column_half = member & 1, member >> 1
    rows = lax.broadcasted_iota(jnp.int32, (8, BLOCK), 0)
    centers = (
        region.astype(f32) + 0.5,
        row_half.astype(f32) + 1.5,
        column_half.astype(f32) + 1.5,
    )
    for index, (row, column) in enumerate(WINDOW):
        row = jnp.where(row_half == 1, 3 - row, row)
        column = jnp.where(column_half == 1, 3 - column, column)
        block = (row & 1) + 2 * (column & 1) + 4 * (row >> 1) + 8 * (column >> 1)
        place = jnp.zeros((8, BLOCK), f32)
        for axis in range(3):
            line = points[axis, pl.ds(block, 1), :] - centers[axis]
            place = jnp.where(rows == axis, jnp.broadcast_to(line, place.shape), place)
        side = right_sides[block]
        sent[index, 0:16, :] = side.astype(bf16)
        high, middle, low = split(place)
        sent[index, 16:32, :] = jnp.concatenate(
            [high + pltpu.roll(low, 3, 0), middle], axis=0
        ).astype(bf16)
        left_rows, right_rows = feature_rows(place)
        left[index] = jnp.transpose(left_rows).astype(bf16)
        if index < 4:
            right[index] = right_rows.astype(bf16)
            own_sides[index] = side
            own_noise[index] = noise_var[pl.ds(block, 1), :]


def neighbour_features(packed, shift):
    rows = lax.broadcasted_iota(jnp.int32, (8, BLOCK), 0)
    packed = packed.astype(f32)
    top, middle = packed[0:8], packed[8:16]
    place = jnp.where(rows < 3, top + middle + pltpu.roll(top, 5, 0), 0.0)
    place = jnp.where(rows == 0, place + shift, place)
    return feature_rows(place)


def sweep(lefts, rights, buffers, use):
    count = len(lefts)

    def distances(step):
        buffers[step % 2][...] = jnp.dot(
            lefts[step](), rights[step](), preferred_element_type=f32
        )

    distances(0)
    for step in range(count):
        if step + 1 < count:
            distances(step + 1)
        parts = []
        for start in range(0, BLOCK, 64):
            squared = jnp.maximum(buffers[step % 2][start:start + 64, :], 1e-30)
            falloff = jnp.maximum(4.0 - squared * lax.rsqrt(squared), 0.0)
            second = falloff * falloff
            parts.append(((second * second) * (5.0 - falloff)).astype(bf16))
        use(step, jnp.concatenate(parts, axis=0))


def times(vectors, tile):
    return jnp.dot(vectors, tile, preferred_element_type=f32)


def times_transposed(vectors, tile):
    return lax.dot_general(vectors, tile, (((1,), (1,)), ((), ())), preferred_element_type=f32)


def within_layer(sent, left, right, totals, tiles, *buffers):
    totals[...] = jnp.zeros_like(totals)
    pairs = SELF + PAIRED + CROSS

    def use(step, tile):
        i, j = pairs[step]
        tiles[step] = tile
        totals[i] += times(sent[j, 0:16, :], tile)
        if i != j and j < 4:
            totals[j] += times_transposed(sent[i, 0:16, :], tile)

    sweep(
        [lambda j=j: left[j] for i, j in pairs],
        [lambda i=i: right[i] for i, j in pairs],
        buffers, use,
    )


def above_own(sent, left, right, above, before, totals, passed, tiles, left_above, right_above, *buffers):
    totals[...] = before[...]
    passed[...] = jnp.zeros_like(passed)
    for j in range(4):
        left_rows, right_rows = neighbour_features(above[j, 16:32, :], 1.0)
        left_above[j] = jnp.transpose(left_rows).astype(bf16)
        right_above[j] = right_rows.astype(bf16)

    def use(step, tile):
        tiles[step] = tile
        if step < 16:
            i, j = step % 4, step // 4
            totals[i] += times(above[j, 0:16, :], tile)
            passed[j] += times_transposed(sent[i, 0:16, :], tile)
        else:
            j, border = CROSS[step - 16]
            passed[j] += times(sent[border, 0:16, :], tile)

    sweep(
        [lambda j=step // 4: left_above[j] for step in range(16)]
        + [lambda border=border: left[border] for j, border in CROSS],
        [lambda i=step % 4: right[i] for step in range(16)]
        + [lambda j=j: right_above[j] for j, border in CROSS],
        buffers, use,
    )


def above_border(right, above, before, totals, left_above, *buffers):
    totals[...] = before[...]
    for j in range(5):
        left_above[j] = jnp.transpose(
            neighbour_features(above[4 + j, 16:32, :], 1.0)[0]
        ).astype(bf16)

    def use(step, tile):
        i, j = CROSS[step]
        totals[i] += times(above[j, 0:16, :], tile)

    sweep(
        [lambda j=j: left_above[j - 4] for i, j in CROSS],
        [lambda i=i: right[i] for i, j in CROSS],
        buffers, use,
    )


def finish_image(totals, arrived, own_noise, own_sides, image, rounded):
    value = (totals[...] + arrived[...]) * (1.0 / 256.0) + own_noise[...] * own_sides[...]
    image[...] = value
    rounded[...] = value.astype(bf16)


def gram(first, second):
    return lax.dot_general(
        first, second, (((1,), (1,)), ((), ())),
        precision=lax.Precision.HIGHEST, preferred_element_type=f32,
    )


def side_by_side(blocks):
    return jnp.concatenate(blocks, axis=1)


def inside(own_sides, image, rounded, own_noise, tiles, products, partial):
    both = jnp.concatenate(
        [side_by_side([image[i] for i in range(4)]), side_by_side([own_sides[i] for i in range(4)])],
        axis=0,
    )
    products[...] = gram(both, both)
    single = [times(rounded[i], tiles[i]) for i in range(4)]
    double = [jnp.zeros((RHS, BLOCK), f32)] * 4
    for step, (i, j) in enumerate(PAIRED):
        double[i] += times(rounded[j], tiles[4 + step])
    for i in range(4):
        partial[i] = own_noise[i] * image[i] * 256.0 + single[i] + 2.0 * double[i]


def outside(from_row, from_column, from_corner, upper, tiles_here, tiles_up, before, image, products, system):
    sources = {4: (from_column, 0), 5: (from_column, 1), 6: (from_row, 0), 7: (from_row, 1), 8: (from_corner, 0)}
    border = {j: ref[place] for j, (ref, place) in sources.items()}
    partial = [before[i] for i in range(4)]
    double = [jnp.zeros((RHS, BLOCK), f32)] * 4
    raised = [jnp.zeros((RHS, BLOCK), f32)] * 4
    for step in range(16):
        double[step % 4] += times(upper[step // 4], tiles_up[step])
    for step, (i, j) in enumerate(CROSS):
        partial[i] += times(border[j], tiles_here[10 + step])
        raised[i] += times(border[j], tiles_up[16 + step])
    third = gram(
        side_by_side([image[i] for i in range(4)] + [upper[i].astype(f32) for i in range(4)]),
        side_by_side([partial[i] + 2.0 * double[i] for i in range(4)] + [2.0 * raised[i] for i in range(4)]),
    ) * (1.0 / 256.0)
    known = products[...]
    second, mixed = known[0:16, 0:16], known[0:16, 16:32]
    crossed, start = known[16:32, 0:16], known[16:32, 16:32]
    top = jnp.concatenate([crossed, second, start, jnp.zeros((RHS, 80), f32)], axis=1)
    bottom = jnp.concatenate([second, third, mixed, jnp.zeros((RHS, 80), f32)], axis=1)
    system[...] = jnp.concatenate([top, bottom], axis=0)


def conclude(system, own_sides, image, result):
    value = system[...]
    lanes = lax.broadcasted_iota(jnp.int32, (32, 128), 1)
    rows = lax.broadcasted_iota(jnp.int32, (32, 128), 0)
    flipped = jnp.transpose(jnp.concatenate([value, jnp.zeros((96, 128), f32)], axis=0))[0:32]
    value = jnp.where(lanes < 32, 0.5 * (value + flipped), value)
    for k in range(0, 32, 2):
        first_column = jnp.broadcast_to(value[:, k:k + 1], value.shape)
        second_column = jnp.broadcast_to(value[:, k + 1:k + 2], value.shape)
        a, b = first_column[k:k + 1], second_column[k:k + 1]
        c, d = first_column[k + 1:k + 2], second_column[k + 1:k + 2]
        first_row, second_row = value[k:k + 1], value[k + 1:k + 2]
        inverse = 1.0 / (a * d - b * c)
        first_new = (d * first_row - b * second_row) * inverse
        second_new = (a * second_row - c * first_row) * inverse
        value = value - first_column * first_new - second_column * second_new
        value = jnp.where(rows == k, first_new, jnp.where(rows == k + 1, second_new, value))
    weights = jnp.transpose(jnp.concatenate([value, jnp.zeros((96, 128), f32)], axis=0))[32:48, 0:32]
    member = lax.axis_index("sub")
    for i, (row, column) in enumerate(OWN):
        both = jnp.concatenate([own_sides[i], image[i]], axis=0)
        place = (row ^ (member & 1)) + 2 * (column ^ (member >> 1))
        result[place] = jnp.dot(
            weights, both, precision=lax.Precision.HIGHEST, preferred_element_type=f32
        )


def local(regions, members, points, noise_var, right_sides, pair_list, pair_count):
    everyone = regions * members

    def from_region(value, step):
        pairs = [
            (source, source - step)
            for source in range(regions)
            if 0 <= source - step < regions
        ]
        return lax.ppermute(value, "region", pairs)

    def from_member(value, mask):
        return lax.ppermute(value, "sub", [(source, source ^ mask) for source in range(members)])

    def sum_over_all(value):
        rounds = [[lambda p, m=m: p ^ m for m in masks] for masks in ((1, 2, 3), (4, 8, 12), (24,))]
        for order in ((1, 0, 3, 2, 5, 4, 7, 6), (7, 2, 1, 4, 3, 6, 5, 0), (3, 6, 5, 0, 7, 2, 1, 4)):
            rounds.append([lambda p, order=order: p % 32 + 32 * order[p // 32]])
        for partners in rounds:
            value = value + sum(
                lax.ppermute(value, ("region", "sub"), [(p, partner(p)) for p in range(everyone)])
                for partner in partners
            )
        return value

    def shape(*dims, dtype=f32):
        return jax.ShapeDtypeStruct(dims, dtype)

    def held(*dims, dtype=bf16):
        return pltpu.VMEM(dims, dtype)

    tile_flops = 2 * BLOCK * BLOCK * 256
    field = (4, RHS, BLOCK)
    buffers = [pltpu.VMEM((BLOCK, BLOCK), f32)] * 2
    sent, left, right, own_sides, own_noise = call(
        prepare, "prepare",
        (shape(9, 32, BLOCK, dtype=bf16), shape(9, BLOCK, FEATURES, dtype=bf16),
         shape(4, FEATURES, BLOCK, dtype=bf16), shape(*field), shape(4, 1, BLOCK)),
        [pltpu.with_memory_space_constraint(value, pltpu.HBM) for value in (points, noise_var, right_sides)],
        tile_flops,
        [pltpu.VMEM(value.shape, f32) for value in (points, noise_var, right_sides)]
        + [pltpu.SemaphoreType.DMA((3,))],
        pltpu.HBM,
    )
    above = from_region(sent, 1)
    totals, tiles_here = call(
        within_layer, "within_layer", (shape(*field), held(19, BLOCK, BLOCK)),
        (sent, left, right), 19 * 4 * tile_flops, buffers,
    )
    totals, passed, tiles_up = call(
        above_own, "above_own", (shape(*field), shape(*field), held(25, BLOCK, BLOCK)),
        (sent, left, right, above, totals), 25 * 4 * tile_flops,
        [pltpu.VMEM((4, BLOCK, FEATURES), bf16), pltpu.VMEM((4, FEATURES, BLOCK), bf16)] + buffers,
    )
    arrived = from_region(passed, -1)
    totals = call(
        above_border, "above_border", shape(*field), (right, above, totals), 9 * 4 * tile_flops,
        [pltpu.VMEM((5, BLOCK, FEATURES), bf16)] + buffers,
    )
    image, rounded = call(
        finish_image, "finish_image", (shape(*field), shape(*field, dtype=bf16)),
        (totals, arrived, own_noise, own_sides), tile_flops // 8,
    )
    upper = from_region(rounded, 1)
    from_row = from_member(rounded[2:4], 1)
    from_column = from_member(rounded[1::2], 2)
    from_corner = from_member(rounded[3:4], 3)
    products, partial = call(
        inside, "inside", (shape(32, 32), shape(*field)),
        (own_sides, image, rounded, own_noise, tiles_here), 10 * 2 * tile_flops,
    )
    system = call(
        outside, "outside", shape(32, 128),
        (from_row, from_column, from_corner, upper, tiles_here, tiles_up, partial, image, products),
        34 * 2 * tile_flops,
    )
    system = sum_over_all(system)
    return call(
        conclude, "conclude", shape(*field), (system, own_sides, image), tile_flops,
    )


def solution(mesh):
    return jax.shard_map(
        functools.partial(local, mesh.shape["region"], mesh.shape["sub"]),
        mesh=mesh,
        in_specs=(
            P(None, "region", None),
            P("region", None),
            P("region", None, None),
            P("region", "sub", None, None),
            P("region", "sub"),
        ),
        out_specs=P(("region", "sub"), None, None),
        check_vma=False,
    )
```

```python
import functools
import jax
import jax.numpy as jnp
from jax import lax
from jax.experimental import pallas as pl
from jax.experimental.pallas import tpu as pltpu
from jax.sharding import PartitionSpec as P

OWN = ((0, 0), (0, 1), (1, 0), (1, 1))
BORDER = ((0, 2), (1, 2), (2, 0), (2, 1), (2, 2))
WINDOW = OWN + BORDER
PAIRED = tuple((i, j) for j in range(4) for i in range(j))
SELF = tuple((i, i) for i in range(4))
CROSS = tuple(
    (i, j)
    for j in range(4, 9)
    for i in range(4)
    if max(abs(OWN[i][0] - WINDOW[j][0]), abs(OWN[i][1] - WINDOW[j][1])) <= 1
)
BLOCK = 512
RHS = 16
FEATURES = 64
f32, bf16 = jnp.float32, jnp.bfloat16
VMEM = pl.BlockSpec(memory_space=pltpu.VMEM)


def call(kernel, name, out_shape, args, flops, scratch=(), args_space=pltpu.VMEM):
    return pl.pallas_call(
        kernel,
        name=name,
        out_shape=out_shape,
        in_specs=[pl.BlockSpec(memory_space=args_space)] * len(args),
        out_specs=jax.tree.map(lambda _: VMEM, out_shape),
        scratch_shapes=scratch,
        compiler_params=pltpu.CompilerParams(vmem_limit_bytes=16 << 20),
        cost_estimate=pl.CostEstimate(flops=flops, bytes_accessed=1 << 20, transcendentals=0),
    )(*args)


def split(value):
    high = value.astype(bf16).astype(f32)
    rest = value - high
    middle = rest.astype(bf16).astype(f32)
    return high, middle, rest - middle


def feature_rows(place):
    rows = lax.broadcasted_iota(jnp.int32, place.shape, 0)
    parts = split(place)
    norms = split(16.0 * jnp.sum(place * place, axis=0, keepdims=True))
    left, right = [], []
    for group, (a, b) in enumerate(((0, 0), (0, 1), (1, 0), (1, 1), (0, 2), (2, 0), (1, 2), (2, 1))):
        one_left, one_right = -32.0 * parts[a], parts[b]
        if group < 3:
            norm = jnp.broadcast_to(norms[group], place.shape)
            one_left = jnp.where(rows == 3, norm, jnp.where(rows == 4, 1.0, one_left))
            one_right = jnp.where(rows == 4, norm, jnp.where(rows == 3, 1.0, one_right))
        left.append(one_left)
        right.append(one_right)
    return jnp.concatenate(left, axis=0), jnp.concatenate(right, axis=0)


def prepare(
    points_far, noise_far, sides_far, sent, left, right, own_sides, own_noise,
    points, noise_var, right_sides, arrivals,
):
    copies = [
        pltpu.make_async_copy(source, target, arrivals.at[place])
        for place, (source, target) in enumerate(
            ((points_far, points), (noise_far, noise_var), (sides_far, right_sides))
        )
    ]
    for copy in copies:
        copy.start()
    for copy in copies:
        copy.wait()
    region = lax.axis_index("region")
    member = lax.axis_index("sub")
    row_half, column_half = member & 1, member >> 1
    rows = lax.broadcasted_iota(jnp.int32, (8, BLOCK), 0)
    centers = (
        region.astype(f32) + 0.5,
        row_half.astype(f32) + 1.5,
        column_half.astype(f32) + 1.5,
    )
    for index, (row, column) in enumerate(WINDOW):
        row = jnp.where(row_half == 1, 3 - row, row)
        column = jnp.where(column_half == 1, 3 - column, column)
        block = (row & 1) + 2 * (column & 1) + 4 * (row >> 1) + 8 * (column >> 1)
        place = jnp.zeros((8, BLOCK), f32)
        for axis in range(3):
            line = points[axis, pl.ds(block, 1), :] - centers[axis]
            place = jnp.where(rows == axis, jnp.broadcast_to(line, place.shape), place)
        side = right_sides[block]
        sent[index, 0:16, :] = side.astype(bf16)
        high, middle, low = split(place)
        sent[index, 16:32, :] = jnp.concatenate(
            [high + pltpu.roll(low, 3, 0), middle], axis=0
        ).astype(bf16)
        left_rows, right_rows = feature_rows(place)
        left[index] = jnp.transpose(left_rows).astype(bf16)
        if index < 4:
            right[index] = right_rows.astype(bf16)
            own_sides[index] = side
            own_noise[index] = noise_var[pl.ds(block, 1), :]


def neighbour_features(packed, shift):
    rows = lax.broadcasted_iota(jnp.int32, (8, BLOCK), 0)
    packed = packed.astype(f32)
    top, middle = packed[0:8], packed[8:16]
    place = jnp.where(rows < 3, top + middle + pltpu.roll(top, 5, 0), 0.0)
    place = jnp.where(rows == 0, place + shift, place)
    return feature_rows(place)


def sweep(lefts, rights, buffers, use):
    count = len(lefts)

    def distances(step):
        buffers[step % 2][...] = jnp.dot(
            lefts[step](), rights[step](), preferred_element_type=f32
        )

    distances(0)
    for step in range(count):
        if step + 1 < count:
            distances(step + 1)
        parts = []
        for start in range(0, BLOCK, 64):
            squared = jnp.maximum(buffers[step % 2][start:start + 64, :], 1e-30)
            falloff = jnp.maximum(4.0 - squared * lax.rsqrt(squared), 0.0)
            second = falloff * falloff
            parts.append(((second * second) * (5.0 - falloff)).astype(bf16))
        use(step, jnp.concatenate(parts, axis=0))


def times(vectors, tile):
    return jnp.dot(vectors, tile, preferred_element_type=f32)


def times_transposed(vectors, tile):
    return lax.dot_general(vectors, tile, (((1,), (1,)), ((), ())), preferred_element_type=f32)


def within_layer(sent, left, right, totals, tiles, *buffers):
    totals[...] = jnp.zeros_like(totals)
    pairs = SELF + PAIRED + CROSS

    def use(step, tile):
        i, j = pairs[step]
        tiles[step] = tile
        totals[i] += times(sent[j, 0:16, :], tile)
        if i != j and j < 4:
            totals[j] += times_transposed(sent[i, 0:16, :], tile)

    sweep(
        [lambda j=j: left[j] for i, j in pairs],
        [lambda i=i: right[i] for i, j in pairs],
        buffers, use,
    )


def above_own(sent, left, right, above, before, totals, passed, tiles, left_above, right_above, *buffers):
    totals[...] = before[...]
    passed[...] = jnp.zeros_like(passed)
    for j in range(4):
        left_rows, right_rows = neighbour_features(above[j, 16:32, :], 1.0)
        left_above[j] = jnp.transpose(left_rows).astype(bf16)
        right_above[j] = right_rows.astype(bf16)

    def use(step, tile):
        tiles[step] = tile
        if step < 16:
            i, j = step % 4, step // 4
            totals[i] += times(above[j, 0:16, :], tile)
            passed[j] += times_transposed(sent[i, 0:16, :], tile)
        else:
            j, border = CROSS[step - 16]
            passed[j] += times(sent[border, 0:16, :], tile)

    sweep(
        [lambda j=step // 4: left_above[j] for step in range(16)]
        + [lambda border=border: left[border] for j, border in CROSS],
        [lambda i=step % 4: right[i] for step in range(16)]
        + [lambda j=j: right_above[j] for j, border in CROSS],
        buffers, use,
    )


def above_border(right, above, before, totals, left_above, *buffers):
    totals[...] = before[...]
    for j in range(5):
        left_above[j] = jnp.transpose(
            neighbour_features(above[4 + j, 16:32, :], 1.0)[0]
        ).astype(bf16)

    def use(step, tile):
        i, j = CROSS[step]
        totals[i] += times(above[j, 0:16, :], tile)

    sweep(
        [lambda j=j: left_above[j - 4] for i, j in CROSS],
        [lambda i=i: right[i] for i, j in CROSS],
        buffers, use,
    )


def finish_image(totals, arrived, own_noise, own_sides, image, rounded):
    value = (totals[...] + arrived[...]) * (1.0 / 256.0) + own_noise[...] * own_sides[...]
    image[...] = value
    rounded[...] = value.astype(bf16)


def gram(first, second):
    return lax.dot_general(
        first, second, (((1,), (1,)), ((), ())),
        precision=lax.Precision.HIGHEST, preferred_element_type=f32,
    )


def side_by_side(blocks):
    return jnp.concatenate(blocks, axis=1)


def inside(own_sides, image, rounded, own_noise, tiles, products, partial):
    both = jnp.concatenate(
        [side_by_side([image[i] for i in range(4)]), side_by_side([own_sides[i] for i in range(4)])],
        axis=0,
    )
    products[...] = gram(both, both)
    single = [times(rounded[i], tiles[i]) for i in range(4)]
    double = [jnp.zeros((RHS, BLOCK), f32)] * 4
    for step, (i, j) in enumerate(PAIRED):
        double[i] += times(rounded[j], tiles[4 + step])
    for i in range(4):
        partial[i] = own_noise[i] * image[i] * 256.0 + single[i] + 2.0 * double[i]


def outside(from_row, from_column, from_corner, upper, tiles_here, tiles_up, before, image, products, copies):
    sources = {4: (from_column, 0), 5: (from_column, 1), 6: (from_row, 0), 7: (from_row, 1), 8: (from_corner, 0)}
    border = {j: ref[place] for j, (ref, place) in sources.items()}
    partial = [before[i] for i in range(4)]
    double = [jnp.zeros((RHS, BLOCK), f32)] * 4
    raised = [jnp.zeros((RHS, BLOCK), f32)] * 4
    for step in range(16):
        double[step % 4] += times(upper[step // 4], tiles_up[step])
    for step, (i, j) in enumerate(CROSS):
        partial[i] += times(border[j], tiles_here[10 + step])
        raised[i] += times(border[j], tiles_up[16 + step])
    third = gram(
        side_by_side([image[i] for i in range(4)] + [upper[i].astype(f32) for i in range(4)]),
        side_by_side([partial[i] + 2.0 * double[i] for i in range(4)] + [2.0 * raised[i] for i in range(4)]),
    ) * (1.0 / 256.0)
    known = products[...]
    ordered = jnp.concatenate(
        [known[16:32, 16:32], known[16:32, 0:16], known[0:16, 0:16], third], axis=1
    )
    packed = jnp.concatenate([ordered[0:8], ordered[8:16]], axis=1)
    copies[...] = jnp.broadcast_to(packed[None], copies.shape)


def add_up(arrived, copies):
    copies[...] = jnp.broadcast_to(jnp.sum(arrived[...], axis=0, keepdims=True), copies.shape)


def conclude(arrived, own_sides, image, result):
    packed = jnp.sum(arrived[...], axis=0)
    ordered = jnp.concatenate([packed[:, 0:64], packed[:, 64:128]], axis=0)
    start, first, second, third = (ordered[:, 16 * part:16 * part + 16] for part in range(4))
    square = jnp.concatenate(
        [jnp.concatenate([first, second], axis=1), jnp.concatenate([second, third], axis=1)], axis=0
    )
    square = jnp.concatenate([square, jnp.zeros((32, 96), f32)], axis=1)
    flipped = jnp.transpose(jnp.concatenate([square, jnp.zeros((96, 128), f32)], axis=0))[0:32]
    square = 0.5 * (square + flipped)
    known = jnp.concatenate([start, square[0:16, 0:16]], axis=0)
    value = jnp.concatenate([square[:, 0:32], known, jnp.zeros((32, 80), f32)], axis=1)
    rows = lax.broadcasted_iota(jnp.int32, (32, 128), 0)
    for k in range(0, 32, 2):
        first_column = jnp.broadcast_to(value[:, k:k + 1], value.shape)
        second_column = jnp.broadcast_to(value[:, k + 1:k + 2], value.shape)
        a, b = first_column[k:k + 1], second_column[k:k + 1]
        c, d = first_column[k + 1:k + 2], second_column[k + 1:k + 2]
        first_row, second_row = value[k:k + 1], value[k + 1:k + 2]
        inverse = 1.0 / (a * d - b * c)
        first_new = (d * first_row - b * second_row) * inverse
        second_new = (a * second_row - c * first_row) * inverse
        value = value - first_column * first_new - second_column * second_new
        value = jnp.where(rows == k, first_new, jnp.where(rows == k + 1, second_new, value))
    weights = jnp.transpose(jnp.concatenate([value, jnp.zeros((96, 128), f32)], axis=0))[32:48, 0:32]
    member = lax.axis_index("sub")
    for i, (row, column) in enumerate(OWN):
        both = jnp.concatenate([own_sides[i], image[i]], axis=0)
        place = (row ^ (member & 1)) + 2 * (column ^ (member >> 1))
        result[place] = jnp.dot(
            weights, both, precision=lax.Precision.HIGHEST, preferred_element_type=f32
        )


def local(regions, members, points, noise_var, right_sides, pair_list, pair_count):
    everyone = regions * members

    def from_region(value, step):
        pairs = [
            (source, source - step)
            for source in range(regions)
            if 0 <= source - step < regions
        ]
        return lax.ppermute(value, "region", pairs)

    def from_member(value, mask):
        return lax.ppermute(value, "sub", [(source, source ^ mask) for source in range(members)])

    def swap(copies, stride):
        size = copies.shape[0]
        groups = [
            [first + stride * place for place in range(size)]
            for first in range(everyone)
            if first // stride % size == 0
        ]
        return lax.all_to_all(
            copies, ("region", "sub"), 0, 0, axis_index_groups=groups, tiled=True
        )

    def shape(*dims, dtype=f32):
        return jax.ShapeDtypeStruct(dims, dtype)

    def held(*dims, dtype=bf16):
        return pltpu.VMEM(dims, dtype)

    tile_flops = 2 * BLOCK * BLOCK * 256
    field = (4, RHS, BLOCK)
    buffers = [pltpu.VMEM((BLOCK, BLOCK), f32)] * 2
    sent, left, right, own_sides, own_noise = call(
        prepare, "prepare",
        (shape(9, 32, BLOCK, dtype=bf16), shape(9, BLOCK, FEATURES, dtype=bf16),
         shape(4, FEATURES, BLOCK, dtype=bf16), shape(*field), shape(4, 1, BLOCK)),
        [pltpu.with_memory_space_constraint(value, pltpu.HBM) for value in (points, noise_var, right_sides)],
        tile_flops,
        [pltpu.VMEM(value.shape, f32) for value in (points, noise_var, right_sides)]
        + [pltpu.SemaphoreType.DMA((3,))],
        pltpu.HBM,
    )
    above = from_region(sent, 1)
    totals, tiles_here = call(
        within_layer, "within_layer", (shape(*field), held(19, BLOCK, BLOCK)),
        (sent, left, right), 19 * 4 * tile_flops, buffers,
    )
    totals, passed, tiles_up = call(
        above_own, "above_own", (shape(*field), shape(*field), held(25, BLOCK, BLOCK)),
        (sent, left, right, above, totals), 25 * 4 * tile_flops,
        [pltpu.VMEM((4, BLOCK, FEATURES), bf16), pltpu.VMEM((4, FEATURES, BLOCK), bf16)] + buffers,
    )
    arrived = from_region(passed, -1)
    totals = call(
        above_border, "above_border", shape(*field), (right, above, totals), 9 * 4 * tile_flops,
        [pltpu.VMEM((5, BLOCK, FEATURES), bf16)] + buffers,
    )
    image, rounded = call(
        finish_image, "finish_image", (shape(*field), shape(*field, dtype=bf16)),
        (totals, arrived, own_noise, own_sides), tile_flops // 8,
    )
    upper = from_region(rounded, 1)
    from_row = from_member(rounded[2:4], 1)
    from_column = from_member(rounded[1::2], 2)
    from_corner = from_member(rounded[3:4], 3)
    products, partial = call(
        inside, "inside", (shape(32, 32), shape(*field)),
        (own_sides, image, rounded, own_noise, tiles_here), 10 * 2 * tile_flops,
    )
    plane = 8 * members
    copies = call(
        outside, "outside", shape(plane, 8, 128),
        (from_row, from_column, from_corner, upper, tiles_here, tiles_up, partial, image, products),
        34 * 2 * tile_flops,
    )
    arrived = swap(copies, 1)
    copies = call(add_up, "add_up", shape(everyone // plane, 8, 128), (arrived,), 1024)
    arrived = swap(copies, plane)
    return call(
        conclude, "conclude", shape(*field), (arrived, own_sides, image), tile_flops,
    )


def solution(mesh):
    return jax.shard_map(
        functools.partial(local, mesh.shape["region"], mesh.shape["sub"]),
        mesh=mesh,
        in_specs=(
            P(None, "region", None),
            P("region", None),
            P("region", None, None),
            P("region", "sub", None, None),
            P("region", "sub"),
        ),
        out_specs=P(("region", "sub"), None, None),
        check_vma=False,
    )
```

```python
import functools
import jax
import jax.numpy as jnp
from jax import lax
from jax.experimental import pallas as pl
from jax.experimental.pallas import tpu as pltpu
from jax.sharding import PartitionSpec as P

OWN = ((0, 0), (0, 1), (1, 0), (1, 1))
BORDER = ((0, 2), (1, 2), (2, 0), (2, 1), (2, 2))
WINDOW = OWN + BORDER
PAIRED = tuple((i, j) for j in range(4) for i in range(j))
SELF = tuple((i, i) for i in range(4))
CROSS = tuple(
    (i, j)
    for j in range(4, 9)
    for i in range(4)
    if max(abs(OWN[i][0] - WINDOW[j][0]), abs(OWN[i][1] - WINDOW[j][1])) <= 1
)
EARLY = SELF + PAIRED + CROSS[:2]
LATE = CROSS[2:]
BLOCK = 512
RHS = 16
FEATURES = 64
f32, bf16 = jnp.float32, jnp.bfloat16
VMEM = pl.BlockSpec(memory_space=pltpu.VMEM)


def call(kernel, name, out_shape, args, flops, scratch=(), args_space=pltpu.VMEM):
    return pl.pallas_call(
        kernel,
        name=name,
        out_shape=out_shape,
        in_specs=[pl.BlockSpec(memory_space=args_space)] * len(args),
        out_specs=jax.tree.map(lambda _: VMEM, out_shape),
        scratch_shapes=scratch,
        compiler_params=pltpu.CompilerParams(vmem_limit_bytes=16 << 20),
        cost_estimate=pl.CostEstimate(flops=flops, bytes_accessed=1 << 20, transcendentals=0),
    )(*args)


def split(value):
    high = value.astype(bf16).astype(f32)
    rest = value - high
    middle = rest.astype(bf16).astype(f32)
    return high, middle, rest - middle


def feature_rows(place):
    rows = lax.broadcasted_iota(jnp.int32, place.shape, 0)
    parts = split(place)
    norms = split(16.0 * jnp.sum(place * place, axis=0, keepdims=True))
    left, right = [], []
    for group, (a, b) in enumerate(((0, 0), (0, 1), (1, 0), (1, 1), (0, 2), (2, 0), (1, 2), (2, 1))):
        one_left, one_right = -32.0 * parts[a], parts[b]
        if group < 3:
            norm = jnp.broadcast_to(norms[group], place.shape)
            one_left = jnp.where(rows == 3, norm, jnp.where(rows == 4, 1.0, one_left))
            one_right = jnp.where(rows == 4, norm, jnp.where(rows == 3, 1.0, one_right))
        left.append(one_left)
        right.append(one_right)
    return jnp.concatenate(left, axis=0), jnp.concatenate(right, axis=0)


def prepare(
    points_far, noise_far, sides_far, sent, left, right, own_sides, own_noise,
    points, noise_var, right_sides, arrivals,
):
    copies = [
        pltpu.make_async_copy(source, target, arrivals.at[place])
        for place, (source, target) in enumerate(
            ((points_far, points), (noise_far, noise_var), (sides_far, right_sides))
        )
    ]
    for copy in copies:
        copy.start()
    copies[0].wait()
    region = lax.axis_index("region")
    member = lax.axis_index("sub")
    row_half, column_half = member & 1, member >> 1
    rows = lax.broadcasted_iota(jnp.int32, (8, BLOCK), 0)
    centers = (
        region.astype(f32) + 0.5,
        row_half.astype(f32) + 1.5,
        column_half.astype(f32) + 1.5,
    )
    blocks = []
    for index, (row, column) in enumerate(WINDOW):
        row = jnp.where(row_half == 1, 3 - row, row)
        column = jnp.where(column_half == 1, 3 - column, column)
        block = (row & 1) + 2 * (column & 1) + 4 * (row >> 1) + 8 * (column >> 1)
        place = jnp.zeros((8, BLOCK), f32)
        for axis in range(3):
            line = points[axis, pl.ds(block, 1), :] - centers[axis]
            place = jnp.where(rows == axis, jnp.broadcast_to(line, place.shape), place)
        blocks.append(block)
        high, middle, low = split(place)
        sent[index, 16:32, :] = jnp.concatenate(
            [high + pltpu.roll(low, 3, 0), middle], axis=0
        ).astype(bf16)
        left_rows, right_rows = feature_rows(place)
        left[index] = jnp.transpose(left_rows).astype(bf16)
        if index < 4:
            right[index] = right_rows.astype(bf16)
    copies[1].wait()
    copies[2].wait()
    for index, block in enumerate(blocks):
        side = right_sides[block]
        sent[index, 0:16, :] = side.astype(bf16)
        if index < 4:
            own_sides[index] = side
            own_noise[index] = noise_var[pl.ds(block, 1), :]


def neighbour_features(packed, shift):
    rows = lax.broadcasted_iota(jnp.int32, (8, BLOCK), 0)
    packed = packed.astype(f32)
    top, middle = packed[0:8], packed[8:16]
    place = jnp.where(rows < 3, top + middle + pltpu.roll(top, 5, 0), 0.0)
    place = jnp.where(rows == 0, place + shift, place)
    return feature_rows(place)


def sweep(lefts, rights, buffers, use):
    count = len(lefts)

    def distances(step):
        buffers[step % 2][...] = jnp.dot(
            lefts[step](), rights[step](), preferred_element_type=f32
        )

    distances(0)
    for step in range(count):
        if step + 1 < count:
            distances(step + 1)
        parts = []
        for start in range(0, BLOCK, 64):
            squared = jnp.maximum(buffers[step % 2][start:start + 64, :], 1e-30)
            falloff = jnp.maximum(4.0 - squared * lax.rsqrt(squared), 0.0)
            second = falloff * falloff
            parts.append(((second * second) * (5.0 - falloff)).astype(bf16))
        use(step, jnp.concatenate(parts, axis=0))


def times(vectors, tile):
    return jnp.dot(vectors, tile, preferred_element_type=f32)


def times_transposed(vectors, tile):
    return lax.dot_general(vectors, tile, (((1,), (1,)), ((), ())), preferred_element_type=f32)


def within_layer(sent, left, right, totals, tiles, *buffers):
    totals[...] = jnp.zeros_like(totals)
    pairs = EARLY

    def use(step, tile):
        i, j = pairs[step]
        tiles[step] = tile
        totals[i] += times(sent[j, 0:16, :], tile)
        if i != j and j < 4:
            totals[j] += times_transposed(sent[i, 0:16, :], tile)

    sweep(
        [lambda j=j: left[j] for i, j in pairs],
        [lambda i=i: right[i] for i, j in pairs],
        buffers, use,
    )


def above_own(sent, left, right, above, before, totals, passed, tiles, left_above, right_above, *buffers):
    totals[...] = before[...]
    passed[...] = jnp.zeros_like(passed)
    for j in range(4):
        left_rows, right_rows = neighbour_features(above[j, 16:32, :], 1.0)
        left_above[j] = jnp.transpose(left_rows).astype(bf16)
        right_above[j] = right_rows.astype(bf16)

    def use(step, tile):
        tiles[step] = tile
        if step < 16:
            i, j = step % 4, step // 4
            totals[i] += times(above[j, 0:16, :], tile)
            passed[j] += times_transposed(sent[i, 0:16, :], tile)
        else:
            j, border = CROSS[step - 16]
            passed[j] += times(sent[border, 0:16, :], tile)

    sweep(
        [lambda j=step // 4: left_above[j] for step in range(16)]
        + [lambda border=border: left[border] for j, border in CROSS],
        [lambda i=step % 4: right[i] for step in range(16)]
        + [lambda j=j: right_above[j] for j, border in CROSS],
        buffers, use,
    )


def borders(sent, left, right, above, before, totals, tiles, left_above, *buffers):
    totals[...] = before[...]
    for j in range(5):
        left_above[j] = jnp.transpose(
            neighbour_features(above[4 + j, 16:32, :], 1.0)[0]
        ).astype(bf16)

    def use(step, tile):
        if step < len(LATE):
            i, j = LATE[step]
            tiles[step] = tile
            totals[i] += times(sent[j, 0:16, :], tile)
        else:
            i, j = CROSS[step - len(LATE)]
            totals[i] += times(above[j, 0:16, :], tile)

    sweep(
        [lambda j=j: left[j] for i, j in LATE] + [lambda j=j: left_above[j - 4] for i, j in CROSS],
        [lambda i=i: right[i] for i, j in LATE + CROSS],
        buffers, use,
    )


def finish_image(totals, arrived, own_noise, own_sides, image, rounded):
    value = (totals[...] + arrived[...]) * (1.0 / 256.0) + own_noise[...] * own_sides[...]
    image[...] = value
    rounded[...] = value.astype(bf16)


def gram(first, second):
    return lax.dot_general(
        first, second, (((1,), (1,)), ((), ())),
        precision=lax.Precision.HIGHEST, preferred_element_type=f32,
    )


def side_by_side(blocks):
    return jnp.concatenate(blocks, axis=1)


def inside(own_sides, image, rounded, own_noise, tiles, products, partial):
    both = jnp.concatenate(
        [side_by_side([image[i] for i in range(4)]), side_by_side([own_sides[i] for i in range(4)])],
        axis=0,
    )
    products[...] = gram(both, both)
    single = [times(rounded[i], tiles[i]) for i in range(4)]
    double = [jnp.zeros((RHS, BLOCK), f32)] * 4
    for step, (i, j) in enumerate(PAIRED):
        double[i] += times(rounded[j], tiles[4 + step])
    for i in range(4):
        partial[i] = own_noise[i] * image[i] * 256.0 + single[i] + 2.0 * double[i]


def upward(upper, tiles, before, partial):
    double = [jnp.zeros((RHS, BLOCK), f32)] * 4
    for step in range(16):
        double[step % 4] += times(upper[step // 4], tiles[step])
    for i in range(4):
        partial[i] = before[i] + 2.0 * double[i]


def outside(from_row, from_column, from_corner, upper, tiles_early, tiles_late, tiles_up, before, image, products, copies):
    sources = {4: (from_column, 0), 5: (from_column, 1), 6: (from_row, 0), 7: (from_row, 1), 8: (from_corner, 0)}
    border = {j: ref[place] for j, (ref, place) in sources.items()}
    single = [jnp.zeros((RHS, BLOCK), f32)] * 4
    raised = [jnp.zeros((RHS, BLOCK), f32)] * 4
    first = len(CROSS) - len(LATE)
    for step, (i, j) in enumerate(CROSS):
        tile = tiles_early[10 + step] if step < first else tiles_late[step - first]
        single[i] += times(border[j], tile)
        raised[i] += times(border[j], tiles_up[16 + step])
    third = gram(
        side_by_side([image[i] for i in range(4)] + [upper[i].astype(f32) for i in range(4)]),
        side_by_side([before[i] + single[i] for i in range(4)] + [2.0 * raised[i] for i in range(4)]),
    ) * (1.0 / 256.0)
    known = products[...]
    ordered = jnp.concatenate(
        [known[16:32, 16:32], known[16:32, 0:16], known[0:16, 0:16], third], axis=1
    )
    packed = jnp.concatenate([ordered[0:8], ordered[8:16]], axis=1)
    copies[...] = jnp.broadcast_to(packed[None], copies.shape)


def add_up(arrived, copies):
    copies[...] = jnp.broadcast_to(jnp.sum(arrived[...], axis=0, keepdims=True), copies.shape)


def conclude(arrived, own_sides, image, result):
    packed = jnp.sum(arrived[...], axis=0)
    ordered = jnp.concatenate([packed[:, 0:64], packed[:, 64:128]], axis=0)
    start, first, second, third = (ordered[:, 16 * part:16 * part + 16] for part in range(4))
    square = jnp.concatenate(
        [jnp.concatenate([first, second], axis=1), jnp.concatenate([second, third], axis=1)], axis=0
    )
    square = jnp.concatenate([square, jnp.zeros((32, 96), f32)], axis=1)
    flipped = jnp.transpose(jnp.concatenate([square, jnp.zeros((96, 128), f32)], axis=0))[0:32]
    square = 0.5 * (square + flipped)
    known = jnp.concatenate([start, square[0:16, 0:16]], axis=0)
    value = jnp.concatenate([square[:, 0:32], known, jnp.zeros((32, 80), f32)], axis=1)
    rows = lax.broadcasted_iota(jnp.int32, (32, 128), 0)
    for k in range(0, 32, 2):
        first_column = jnp.broadcast_to(value[:, k:k + 1], value.shape)
        second_column = jnp.broadcast_to(value[:, k + 1:k + 2], value.shape)
        a, b = first_column[k:k + 1], second_column[k:k + 1]
        c, d = first_column[k + 1:k + 2], second_column[k + 1:k + 2]
        first_row, second_row = value[k:k + 1], value[k + 1:k + 2]
        inverse = 1.0 / (a * d - b * c)
        first_new = (d * first_row - b * second_row) * inverse
        second_new = (a * second_row - c * first_row) * inverse
        value = value - first_column * first_new - second_column * second_new
        value = jnp.where(rows == k, first_new, jnp.where(rows == k + 1, second_new, value))
    weights = jnp.transpose(jnp.concatenate([value, jnp.zeros((96, 128), f32)], axis=0))[32:48, 0:32]
    member = lax.axis_index("sub")
    for i, (row, column) in enumerate(OWN):
        both = jnp.concatenate([own_sides[i], image[i]], axis=0)
        place = (row ^ (member & 1)) + 2 * (column ^ (member >> 1))
        result[place] = jnp.dot(
            weights, both, precision=lax.Precision.HIGHEST, preferred_element_type=f32
        )


def local(regions, members, points, noise_var, right_sides, pair_list, pair_count):
    everyone = regions * members

    def from_region(value, step):
        pairs = [
            (source, source - step)
            for source in range(regions)
            if 0 <= source - step < regions
        ]
        return lax.ppermute(value, "region", pairs)

    def from_member(value, mask):
        return lax.ppermute(value, "sub", [(source, source ^ mask) for source in range(members)])

    def swap(copies, stride):
        size = copies.shape[0]
        groups = [
            [first + stride * place for place in range(size)]
            for first in range(everyone)
            if first // stride % size == 0
        ]
        return lax.all_to_all(
            copies, ("region", "sub"), 0, 0, axis_index_groups=groups, tiled=True
        )

    def shape(*dims, dtype=f32):
        return jax.ShapeDtypeStruct(dims, dtype)

    def held(*dims, dtype=bf16):
        return pltpu.VMEM(dims, dtype)

    tile_flops = 2 * BLOCK * BLOCK * 256
    field = (4, RHS, BLOCK)
    buffers = [pltpu.VMEM((BLOCK, BLOCK), f32)] * 2
    sent, left, right, own_sides, own_noise = call(
        prepare, "prepare",
        (shape(9, 32, BLOCK, dtype=bf16), shape(9, BLOCK, FEATURES, dtype=bf16),
         shape(4, FEATURES, BLOCK, dtype=bf16), shape(*field), shape(4, 1, BLOCK)),
        [pltpu.with_memory_space_constraint(value, pltpu.HBM) for value in (points, noise_var, right_sides)],
        tile_flops,
        [pltpu.VMEM(value.shape, f32) for value in (points, noise_var, right_sides)]
        + [pltpu.SemaphoreType.DMA((3,))],
        pltpu.HBM,
    )
    above = from_region(sent, 1)
    totals, tiles_early = call(
        within_layer, "within_layer", (shape(*field), held(len(EARLY), BLOCK, BLOCK)),
        (sent, left, right), len(EARLY) * 4 * tile_flops, buffers,
    )
    totals, passed, tiles_up = call(
        above_own, "above_own", (shape(*field), shape(*field), held(25, BLOCK, BLOCK)),
        (sent, left, right, above, totals), 25 * 4 * tile_flops,
        [pltpu.VMEM((4, BLOCK, FEATURES), bf16), pltpu.VMEM((4, FEATURES, BLOCK), bf16)] + buffers,
    )
    arrived = from_region(passed, -1)
    totals, tiles_late = call(
        borders, "borders", (shape(*field), held(len(LATE), BLOCK, BLOCK)),
        (sent, left, right, above, totals), 16 * 4 * tile_flops,
        [pltpu.VMEM((5, BLOCK, FEATURES), bf16)] + buffers,
    )
    image, rounded = call(
        finish_image, "finish_image", (shape(*field), shape(*field, dtype=bf16)),
        (totals, arrived, own_noise, own_sides), tile_flops // 8,
    )
    upper = from_region(rounded, 1)
    from_row = from_member(rounded[2:4], 1)
    from_column = from_member(rounded[1::2], 2)
    from_corner = from_member(rounded[3:4], 3)
    products, partial = call(
        inside, "inside", (shape(32, 32), shape(*field)),
        (own_sides, image, rounded, own_noise, tiles_early), 10 * 2 * tile_flops,
    )
    partial = call(
        upward, "upward", shape(*field), (upper, tiles_up, partial), 16 * 2 * tile_flops,
    )
    plane = 8 * members
    copies = call(
        outside, "outside", shape(plane, 8, 128),
        (from_row, from_column, from_corner, upper, tiles_early, tiles_late, tiles_up, partial,
         image, products),
        18 * 2 * tile_flops,
    )
    arrived = swap(copies, 1)
    copies = call(add_up, "add_up", shape(everyone // plane, 8, 128), (arrived,), 1024)
    arrived = swap(copies, plane)
    return call(
        conclude, "conclude", shape(*field), (arrived, own_sides, image), tile_flops,
    )


def solution(mesh):
    return jax.shard_map(
        functools.partial(local, mesh.shape["region"], mesh.shape["sub"]),
        mesh=mesh,
        in_specs=(
            P(None, "region", None),
            P("region", None),
            P("region", None, None),
            P("region", "sub", None, None),
            P("region", "sub"),
        ),
        out_specs=P(("region", "sub"), None, None),
        check_vma=False,
    )
```

```python
import functools
import jax
import jax.numpy as jnp
from jax import lax
from jax.experimental import pallas as pl
from jax.experimental.pallas import tpu as pltpu
from jax.sharding import PartitionSpec as P

OWN = ((0, 0), (0, 1), (1, 0), (1, 1))
BORDER = ((0, 2), (1, 2), (2, 0), (2, 1), (2, 2))
WINDOW = OWN + BORDER
PAIRED = tuple((i, j) for j in range(4) for i in range(j))
SELF = tuple((i, i) for i in range(4))
CROSS = tuple(
    (i, j)
    for j in range(4, 9)
    for i in range(4)
    if max(abs(OWN[i][0] - WINDOW[j][0]), abs(OWN[i][1] - WINDOW[j][1])) <= 1
)
EARLY = SELF + PAIRED + CROSS[:6]
LATE = CROSS[6:]
BLOCK = 512
RHS = 16
FEATURES = 64
f32, bf16 = jnp.float32, jnp.bfloat16
VMEM = pl.BlockSpec(memory_space=pltpu.VMEM)


def call(kernel, name, out_shape, args, flops, scratch=(), args_space=pltpu.VMEM):
    return pl.pallas_call(
        kernel,
        name=name,
        out_shape=out_shape,
        in_specs=[pl.BlockSpec(memory_space=args_space)] * len(args),
        out_specs=jax.tree.map(lambda _: VMEM, out_shape),
        scratch_shapes=scratch,
        compiler_params=pltpu.CompilerParams(vmem_limit_bytes=16 << 20),
        cost_estimate=pl.CostEstimate(flops=flops, bytes_accessed=1 << 20, transcendentals=0),
    )(*args)


def split(value):
    high = value.astype(bf16).astype(f32)
    rest = value - high
    middle = rest.astype(bf16).astype(f32)
    return high, middle, rest - middle


def feature_rows(place):
    rows = lax.broadcasted_iota(jnp.int32, place.shape, 0)
    parts = split(place)
    norms = split(16.0 * jnp.sum(place * place, axis=0, keepdims=True))
    left, right = [], []
    for group, (a, b) in enumerate(((0, 0), (0, 1), (1, 0), (1, 1), (0, 2), (2, 0), (1, 2), (2, 1))):
        one_left, one_right = -32.0 * parts[a], parts[b]
        if group < 3:
            norm = jnp.broadcast_to(norms[group], place.shape)
            one_left = jnp.where(rows == 3, norm, jnp.where(rows == 4, 1.0, one_left))
            one_right = jnp.where(rows == 4, norm, jnp.where(rows == 3, 1.0, one_right))
        left.append(one_left)
        right.append(one_right)
    return jnp.concatenate(left, axis=0), jnp.concatenate(right, axis=0)


def prepare(
    points_far, noise_far, sides_far, sent, left, right, own_sides, own_noise,
    points, noise_var, right_sides, arrivals,
):
    copies = [
        pltpu.make_async_copy(source, target, arrivals.at[place])
        for place, (source, target) in enumerate(
            ((points_far, points), (noise_far, noise_var), (sides_far, right_sides))
        )
    ]
    for copy in copies:
        copy.start()
    copies[0].wait()
    region = lax.axis_index("region")
    member = lax.axis_index("sub")
    row_half, column_half = member & 1, member >> 1
    rows = lax.broadcasted_iota(jnp.int32, (8, BLOCK), 0)
    centers = (
        region.astype(f32) + 0.5,
        row_half.astype(f32) + 1.5,
        column_half.astype(f32) + 1.5,
    )
    blocks = []
    for index, (row, column) in enumerate(WINDOW):
        row = jnp.where(row_half == 1, 3 - row, row)
        column = jnp.where(column_half == 1, 3 - column, column)
        block = (row & 1) + 2 * (column & 1) + 4 * (row >> 1) + 8 * (column >> 1)
        place = jnp.zeros((8, BLOCK), f32)
        for axis in range(3):
            line = points[axis, pl.ds(block, 1), :] - centers[axis]
            place = jnp.where(rows == axis, jnp.broadcast_to(line, place.shape), place)
        blocks.append(block)
        high, middle, low = split(place)
        sent[index, 16:32, :] = jnp.concatenate(
            [high + pltpu.roll(low, 3, 0), middle], axis=0
        ).astype(bf16)
        left_rows, right_rows = feature_rows(place)
        left[index] = jnp.transpose(left_rows).astype(bf16)
        if index < 4:
            right[index] = right_rows.astype(bf16)
    copies[1].wait()
    copies[2].wait()
    for index, block in enumerate(blocks):
        side = right_sides[block]
        sent[index, 0:16, :] = side.astype(bf16)
        if index < 4:
            own_sides[index] = side
            own_noise[index] = noise_var[pl.ds(block, 1), :]


def neighbour_features(packed, shift):
    rows = lax.broadcasted_iota(jnp.int32, (8, BLOCK), 0)
    packed = packed.astype(f32)
    top, middle = packed[0:8], packed[8:16]
    place = jnp.where(rows < 3, top + middle + pltpu.roll(top, 5, 0), 0.0)
    place = jnp.where(rows == 0, place + shift, place)
    return feature_rows(place)


def sweep(lefts, rights, buffers, use):
    count = len(lefts)

    def distances(step):
        buffers[step % 2][...] = jnp.dot(
            lefts[step](), rights[step](), preferred_element_type=f32
        )

    distances(0)
    for step in range(count):
        if step + 1 < count:
            distances(step + 1)
        parts = []
        for start in range(0, BLOCK, 64):
            squared = jnp.maximum(buffers[step % 2][start:start + 64, :], 1e-30)
            falloff = jnp.maximum(4.0 - squared * lax.rsqrt(squared), 0.0)
            second = falloff * falloff
            parts.append(((second * second) * (5.0 - falloff)).astype(bf16))
        use(step, jnp.concatenate(parts, axis=0))


def times(vectors, tile):
    return jnp.dot(vectors, tile, preferred_element_type=f32)


def times_transposed(vectors, tile):
    return lax.dot_general(vectors, tile, (((1,), (1,)), ((), ())), preferred_element_type=f32)


def within_layer(sent, left, right, totals, tiles, *buffers):
    totals[...] = jnp.zeros_like(totals)
    pairs = EARLY

    def use(step, tile):
        i, j = pairs[step]
        tiles[step] = tile
        totals[i] += times(sent[j, 0:16, :], tile)
        if i != j and j < 4:
            totals[j] += times_transposed(sent[i, 0:16, :], tile)

    sweep(
        [lambda j=j: left[j] for i, j in pairs],
        [lambda i=i: right[i] for i, j in pairs],
        buffers, use,
    )


def above_own(
    sent, left, right, above, before, totals, leaving, tiles,
    left_above, right_above, passed, *buffers,
):
    totals[...] = before[...]
    passed[...] = jnp.zeros_like(passed)
    for j in range(4):
        left_rows, right_rows = neighbour_features(above[j, 16:32, :], 1.0)
        left_above[j] = jnp.transpose(left_rows).astype(bf16)
        right_above[j] = right_rows.astype(bf16)

    def use(step, tile):
        tiles[step] = tile
        if step < 16:
            i, j = step % 4, step // 4
            totals[i] += times(above[j, 0:16, :], tile)
            passed[j] += times_transposed(sent[i, 0:16, :], tile)
        else:
            j, border = CROSS[step - 16]
            passed[j] += times(sent[border, 0:16, :], tile)

    sweep(
        [lambda j=step // 4: left_above[j] for step in range(16)]
        + [lambda border=border: left[border] for j, border in CROSS],
        [lambda i=step % 4: right[i] for step in range(16)]
        + [lambda j=j: right_above[j] for j, border in CROSS],
        buffers, use,
    )
    leaving[...] = passed[...].astype(bf16)


def borders(sent, left, right, above, before, totals, tiles, left_above, *buffers):
    totals[...] = before[...]
    for j in range(5):
        left_above[j] = jnp.transpose(
            neighbour_features(above[4 + j, 16:32, :], 1.0)[0]
        ).astype(bf16)

    def use(step, tile):
        if step < len(LATE):
            i, j = LATE[step]
            tiles[step] = tile
            totals[i] += times(sent[j, 0:16, :], tile)
        else:
            i, j = CROSS[step - len(LATE)]
            totals[i] += times(above[j, 0:16, :], tile)

    sweep(
        [lambda j=j: left[j] for i, j in LATE] + [lambda j=j: left_above[j - 4] for i, j in CROSS],
        [lambda i=i: right[i] for i, j in LATE + CROSS],
        buffers, use,
    )


def finish_image(totals, arrived, own_noise, own_sides, image, rounded):
    value = (totals[...] + arrived[...].astype(f32)) * (1.0 / 256.0) + own_noise[...] * own_sides[...]
    image[...] = value
    rounded[...] = value.astype(bf16)


def gram(first, second):
    return lax.dot_general(
        first, second, (((1,), (1,)), ((), ())),
        precision=lax.Precision.HIGHEST, preferred_element_type=f32,
    )


def side_by_side(blocks):
    return jnp.concatenate(blocks, axis=1)


def inside(own_sides, image, rounded, own_noise, tiles, products, partial):
    both = jnp.concatenate(
        [side_by_side([image[i] for i in range(4)]), side_by_side([own_sides[i] for i in range(4)])],
        axis=0,
    )
    products[...] = gram(both, both)
    single = [times(rounded[i], tiles[i]) for i in range(4)]
    double = [jnp.zeros((RHS, BLOCK), f32)] * 4
    for step, (i, j) in enumerate(PAIRED):
        double[i] += times(rounded[j], tiles[4 + step])
    for i in range(4):
        partial[i] = own_noise[i] * image[i] * 256.0 + single[i] + 2.0 * double[i]


def upward(upper, tiles, before, partial):
    double = [jnp.zeros((RHS, BLOCK), f32)] * 4
    for step in range(16):
        double[step % 4] += times(upper[step // 4], tiles[step])
    for i in range(4):
        partial[i] = before[i] + 2.0 * double[i]


def outside(from_row, from_column, from_corner, upper, tiles_early, tiles_late, tiles_up, before, image, products, copies):
    sources = {4: (from_column, 0), 5: (from_column, 1), 6: (from_row, 0), 7: (from_row, 1), 8: (from_corner, 0)}
    border = {j: ref[place] for j, (ref, place) in sources.items()}
    single = [jnp.zeros((RHS, BLOCK), f32)] * 4
    raised = [jnp.zeros((RHS, BLOCK), f32)] * 4
    first = len(CROSS) - len(LATE)
    for step, (i, j) in enumerate(CROSS):
        tile = tiles_early[10 + step] if step < first else tiles_late[step - first]
        single[i] += times(border[j], tile)
        raised[i] += times(border[j], tiles_up[16 + step])
    third = gram(
        side_by_side([image[i] for i in range(4)] + [upper[i].astype(f32) for i in range(4)]),
        side_by_side([before[i] + single[i] for i in range(4)] + [2.0 * raised[i] for i in range(4)]),
    ) * (1.0 / 256.0)
    known = products[...]
    ordered = jnp.concatenate(
        [known[16:32, 16:32], known[16:32, 0:16], known[0:16, 0:16], third], axis=1
    )
    packed = jnp.concatenate([ordered[0:8], ordered[8:16]], axis=1)
    copies[...] = jnp.broadcast_to(packed[None], copies.shape)


def add_up(arrived, copies):
    copies[...] = jnp.broadcast_to(jnp.sum(arrived[...], axis=0, keepdims=True), copies.shape)


def conclude(arrived, own_sides, image, result):
    packed = jnp.sum(arrived[...], axis=0)
    ordered = jnp.concatenate([packed[:, 0:64], packed[:, 64:128]], axis=0)
    start, first, second, third = (ordered[:, 16 * part:16 * part + 16] for part in range(4))
    square = jnp.concatenate(
        [jnp.concatenate([first, second], axis=1), jnp.concatenate([second, third], axis=1)], axis=0
    )
    square = jnp.concatenate([square, jnp.zeros((32, 96), f32)], axis=1)
    flipped = jnp.transpose(jnp.concatenate([square, jnp.zeros((96, 128), f32)], axis=0))[0:32]
    square = 0.5 * (square + flipped)
    known = jnp.concatenate([start, square[0:16, 0:16]], axis=0)
    value = jnp.concatenate([square[:, 0:32], known, jnp.zeros((32, 80), f32)], axis=1)
    rows = lax.broadcasted_iota(jnp.int32, (32, 128), 0)
    for k in range(0, 32, 2):
        first_column = jnp.broadcast_to(value[:, k:k + 1], value.shape)
        second_column = jnp.broadcast_to(value[:, k + 1:k + 2], value.shape)
        a, b = first_column[k:k + 1], second_column[k:k + 1]
        c, d = first_column[k + 1:k + 2], second_column[k + 1:k + 2]
        first_row, second_row = value[k:k + 1], value[k + 1:k + 2]
        inverse = 1.0 / (a * d - b * c)
        first_new = (d * first_row - b * second_row) * inverse
        second_new = (a * second_row - c * first_row) * inverse
        value = value - first_column * first_new - second_column * second_new
        value = jnp.where(rows == k, first_new, jnp.where(rows == k + 1, second_new, value))
    weights = jnp.transpose(jnp.concatenate([value, jnp.zeros((96, 128), f32)], axis=0))[32:48, 0:32]
    member = lax.axis_index("sub")
    for i, (row, column) in enumerate(OWN):
        both = jnp.concatenate([own_sides[i], image[i]], axis=0)
        place = (row ^ (member & 1)) + 2 * (column ^ (member >> 1))
        result[place] = jnp.dot(
            weights, both, precision=lax.Precision.HIGHEST, preferred_element_type=f32
        )


def local(regions, members, points, noise_var, right_sides, pair_list, pair_count):
    everyone = regions * members

    def from_region(value, step):
        pairs = [
            (source, source - step)
            for source in range(regions)
            if 0 <= source - step < regions
        ]
        return lax.ppermute(value, "region", pairs)

    def from_member(value, mask):
        return lax.ppermute(value, "sub", [(source, source ^ mask) for source in range(members)])

    def swap(copies, stride):
        size = copies.shape[0]
        groups = [
            [first + stride * place for place in range(size)]
            for first in range(everyone)
            if first // stride % size == 0
        ]
        return lax.all_to_all(
            copies, ("region", "sub"), 0, 0, axis_index_groups=groups, tiled=True
        )

    def shape(*dims, dtype=f32):
        return jax.ShapeDtypeStruct(dims, dtype)

    def held(*dims, dtype=bf16):
        return pltpu.VMEM(dims, dtype)

    tile_flops = 2 * BLOCK * BLOCK * 256
    field = (4, RHS, BLOCK)
    buffers = [pltpu.VMEM((BLOCK, BLOCK), f32)] * 2
    sent, left, right, own_sides, own_noise = call(
        prepare, "prepare",
        (shape(9, 32, BLOCK, dtype=bf16), shape(9, BLOCK, FEATURES, dtype=bf16),
         shape(4, FEATURES, BLOCK, dtype=bf16), shape(*field), shape(4, 1, BLOCK)),
        [pltpu.with_memory_space_constraint(value, pltpu.HBM) for value in (points, noise_var, right_sides)],
        tile_flops,
        [pltpu.VMEM(value.shape, f32) for value in (points, noise_var, right_sides)]
        + [pltpu.SemaphoreType.DMA((3,))],
        pltpu.HBM,
    )
    above = from_region(sent, 1)
    totals, tiles_early = call(
        within_layer, "within_layer", (shape(*field), held(len(EARLY), BLOCK, BLOCK)),
        (sent, left, right), len(EARLY) * 4 * tile_flops, buffers,
    )
    totals, passed, tiles_up = call(
        above_own, "above_own",
        (shape(*field), shape(*field, dtype=bf16), held(25, BLOCK, BLOCK)),
        (sent, left, right, above, totals), 25 * 4 * tile_flops,
        [pltpu.VMEM((4, BLOCK, FEATURES), bf16), pltpu.VMEM((4, FEATURES, BLOCK), bf16),
         pltpu.VMEM(field, f32)] + buffers,
    )
    arrived = from_region(passed, -1)
    totals, tiles_late = call(
        borders, "borders", (shape(*field), held(len(LATE), BLOCK, BLOCK)),
        (sent, left, right, above, totals), 16 * 4 * tile_flops,
        [pltpu.VMEM((5, BLOCK, FEATURES), bf16)] + buffers,
    )
    image, rounded = call(
        finish_image, "finish_image", (shape(*field), shape(*field, dtype=bf16)),
        (totals, arrived, own_noise, own_sides), tile_flops // 8,
    )
    upper = from_region(rounded, 1)
    from_row = from_member(rounded[2:4], 1)
    from_column = from_member(rounded[1::2], 2)
    from_corner = from_member(rounded[3:4], 3)
    products, partial = call(
        inside, "inside", (shape(32, 32), shape(*field)),
        (own_sides, image, rounded, own_noise, tiles_early), 10 * 2 * tile_flops,
    )
    partial = call(
        upward, "upward", shape(*field), (upper, tiles_up, partial), 16 * 2 * tile_flops,
    )
    plane = 8 * members
    copies = call(
        outside, "outside", shape(plane, 8, 128),
        (from_row, from_column, from_corner, upper, tiles_early, tiles_late, tiles_up, partial,
         image, products),
        18 * 2 * tile_flops,
    )
    arrived = swap(copies, 1)
    copies = call(add_up, "add_up", shape(everyone // plane, 8, 128), (arrived,), 1024)
    arrived = swap(copies, plane)
    return call(
        conclude, "conclude", shape(*field), (arrived, own_sides, image), tile_flops,
    )


def solution(mesh):
    return jax.shard_map(
        functools.partial(local, mesh.shape["region"], mesh.shape["sub"]),
        mesh=mesh,
        in_specs=(
            P(None, "region", None),
            P("region", None),
            P("region", None, None),
            P("region", "sub", None, None),
            P("region", "sub"),
        ),
        out_specs=P(("region", "sub"), None, None),
        check_vma=False,
    )
```

```python
import functools
import jax
import jax.numpy as jnp
from jax import lax
from jax.experimental import pallas as pl
from jax.experimental.pallas import tpu as pltpu
from jax.sharding import PartitionSpec as P

OWN = ((0, 0), (0, 1), (1, 0), (1, 1))
BORDER = ((0, 2), (1, 2), (2, 0), (2, 1), (2, 2))
WINDOW = OWN + BORDER
PAIRED = tuple((i, j) for j in range(4) for i in range(j))
SELF = tuple((i, i) for i in range(4))
CROSS = tuple(
    (i, j)
    for j in range(4, 9)
    for i in range(4)
    if max(abs(OWN[i][0] - WINDOW[j][0]), abs(OWN[i][1] - WINDOW[j][1])) <= 1
)
EARLY = SELF + PAIRED + CROSS[:6]
LATE = CROSS[6:]
BLOCK = 512
RHS = 16
FEATURES = 64
f32, bf16 = jnp.float32, jnp.bfloat16
VMEM = pl.BlockSpec(memory_space=pltpu.VMEM)


def call(kernel, name, out_shape, args, flops, scratch=(), args_space=pltpu.VMEM):
    return pl.pallas_call(
        kernel,
        name=name,
        out_shape=out_shape,
        in_specs=[pl.BlockSpec(memory_space=args_space)] * len(args),
        out_specs=jax.tree.map(lambda _: VMEM, out_shape),
        scratch_shapes=scratch,
        compiler_params=pltpu.CompilerParams(vmem_limit_bytes=16 << 20),
        cost_estimate=pl.CostEstimate(flops=flops, bytes_accessed=1 << 20, transcendentals=0),
    )(*args)


def split(value):
    high = value.astype(bf16).astype(f32)
    rest = value - high
    middle = rest.astype(bf16).astype(f32)
    return high, middle, rest - middle


def feature_rows(place):
    rows = lax.broadcasted_iota(jnp.int32, place.shape, 0)
    parts = split(place)
    norms = split(16.0 * jnp.sum(place * place, axis=0, keepdims=True))
    left, right = [], []
    for group, (a, b) in enumerate(((0, 0), (0, 1), (1, 0), (1, 1), (0, 2), (2, 0), (1, 2), (2, 1))):
        one_left, one_right = -32.0 * parts[a], parts[b]
        if group < 3:
            norm = jnp.broadcast_to(norms[group], place.shape)
            one_left = jnp.where(rows == 3, norm, jnp.where(rows == 4, 1.0, one_left))
            one_right = jnp.where(rows == 4, norm, jnp.where(rows == 3, 1.0, one_right))
        left.append(one_left)
        right.append(one_right)
    return jnp.concatenate(left, axis=0), jnp.concatenate(right, axis=0)


def prepare(
    points_far, noise_far, sides_far, sent, left, right, own_sides, own_noise,
    points, noise_var, right_sides, arrivals,
):
    copies = [
        pltpu.make_async_copy(source, target, arrivals.at[place])
        for place, (source, target) in enumerate(
            ((points_far, points), (noise_far, noise_var), (sides_far, right_sides))
        )
    ]
    for copy in copies:
        copy.start()
    copies[0].wait()
    region = lax.axis_index("region")
    member = lax.axis_index("sub")
    row_half, column_half = member & 1, member >> 1
    rows = lax.broadcasted_iota(jnp.int32, (8, BLOCK), 0)
    centers = (
        region.astype(f32) + 0.5,
        row_half.astype(f32) + 1.5,
        column_half.astype(f32) + 1.5,
    )
    blocks = []
    for index, (row, column) in enumerate(WINDOW):
        row = jnp.where(row_half == 1, 3 - row, row)
        column = jnp.where(column_half == 1, 3 - column, column)
        block = (row & 1) + 2 * (column & 1) + 4 * (row >> 1) + 8 * (column >> 1)
        place = jnp.zeros((8, BLOCK), f32)
        for axis in range(3):
            line = points[axis, pl.ds(block, 1), :] - centers[axis]
            place = jnp.where(rows == axis, jnp.broadcast_to(line, place.shape), place)
        blocks.append(block)
        high, middle, low = split(place)
        sent[index, 16:32, :] = jnp.concatenate(
            [high + pltpu.roll(low, 3, 0), middle], axis=0
        ).astype(bf16)
        left_rows, right_rows = feature_rows(place)
        left[index] = jnp.transpose(left_rows).astype(bf16)
        if index < 4:
            right[index] = right_rows.astype(bf16)
    copies[1].wait()
    copies[2].wait()
    for index, block in enumerate(blocks):
        side = right_sides[block]
        sent[index, 0:16, :] = side.astype(bf16)
        if index < 4:
            own_sides[index] = side
            own_noise[index] = noise_var[pl.ds(block, 1), :]


def neighbour_features(packed, shift):
    rows = lax.broadcasted_iota(jnp.int32, (8, BLOCK), 0)
    packed = packed.astype(f32)
    top, middle = packed[0:8], packed[8:16]
    place = jnp.where(rows < 3, top + middle + pltpu.roll(top, 5, 0), 0.0)
    place = jnp.where(rows == 0, place + shift, place)
    return feature_rows(place)


def sweep(lefts, rights, buffers, use):
    count = len(lefts)

    def distances(step):
        buffers[step % 2][...] = jnp.dot(
            lefts[step](), rights[step](), preferred_element_type=f32
        )

    distances(0)
    for step in range(count):
        if step + 1 < count:
            distances(step + 1)
        parts = []
        for start in range(0, BLOCK, 64):
            squared = jnp.maximum(buffers[step % 2][start:start + 64, :], 1e-30)
            falloff = jnp.maximum(4.0 - squared * lax.rsqrt(squared), 0.0)
            second = falloff * falloff
            parts.append(((second * second) * (5.0 - falloff)).astype(bf16))
        use(step, jnp.concatenate(parts, axis=0))


def times(vectors, tile):
    return jnp.dot(vectors, tile, preferred_element_type=f32)


def times_transposed(vectors, tile):
    return lax.dot_general(vectors, tile, (((1,), (1,)), ((), ())), preferred_element_type=f32)


def within_layer(sent, left, right, totals, tiles, *buffers):
    totals[...] = jnp.zeros_like(totals)
    pairs = EARLY

    def use(step, tile):
        i, j = pairs[step]
        tiles[step] = tile
        totals[i] += times(sent[j, 0:16, :], tile)
        if i != j and j < 4:
            totals[j] += times_transposed(sent[i, 0:16, :], tile)

    sweep(
        [lambda j=j: left[j] for i, j in pairs],
        [lambda i=i: right[i] for i, j in pairs],
        buffers, use,
    )


def above_own(
    sent, left, right, above, before, totals, leaving, tiles,
    left_above, right_above, passed, *buffers,
):
    totals[...] = before[...]
    passed[...] = jnp.zeros_like(passed)
    for j in range(4):
        left_rows, right_rows = neighbour_features(above[j, 16:32, :], 1.0)
        left_above[j] = jnp.transpose(left_rows).astype(bf16)
        right_above[j] = right_rows.astype(bf16)

    def use(step, tile):
        tiles[step] = tile
        if step < 16:
            i, j = step % 4, step // 4
            totals[i] += times(above[j, 0:16, :], tile)
            passed[j] += times_transposed(sent[i, 0:16, :], tile)
        else:
            j, border = CROSS[step - 16]
            passed[j] += times(sent[border, 0:16, :], tile)

    sweep(
        [lambda j=step // 4: left_above[j] for step in range(16)]
        + [lambda border=border: left[border] for j, border in CROSS],
        [lambda i=step % 4: right[i] for step in range(16)]
        + [lambda j=j: right_above[j] for j, border in CROSS],
        buffers, use,
    )
    leaving[...] = passed[...].astype(bf16)


def borders(sent, left, right, above, before, totals, tiles, left_above, *buffers):
    totals[...] = before[...]
    for j in range(5):
        left_above[j] = jnp.transpose(
            neighbour_features(above[4 + j, 16:32, :], 1.0)[0]
        ).astype(bf16)

    def use(step, tile):
        if step < len(LATE):
            i, j = LATE[step]
            tiles[step] = tile
            totals[i] += times(sent[j, 0:16, :], tile)
        else:
            i, j = CROSS[step - len(LATE)]
            totals[i] += times(above[j, 0:16, :], tile)

    sweep(
        [lambda j=j: left[j] for i, j in LATE] + [lambda j=j: left_above[j - 4] for i, j in CROSS],
        [lambda i=i: right[i] for i, j in LATE + CROSS],
        buffers, use,
    )


def finish_image(totals, arrived, own_noise, own_sides, image, rounded):
    value = (totals[...] + arrived[...].astype(f32)) * (1.0 / 256.0) + own_noise[...] * own_sides[...]
    image[...] = value
    rounded[...] = value.astype(bf16)


def gram(first, second):
    return lax.dot_general(
        first, second, (((1,), (1,)), ((), ())),
        precision=lax.Precision.HIGHEST, preferred_element_type=f32,
    )


def side_by_side(blocks):
    return jnp.concatenate(blocks, axis=1)


def inside(own_sides, image, rounded, own_noise, tiles, products, partial):
    both = jnp.concatenate(
        [side_by_side([image[i] for i in range(4)]), side_by_side([own_sides[i] for i in range(4)])],
        axis=0,
    )
    products[...] = gram(both, both)
    single = [times(rounded[i], tiles[i]) for i in range(4)]
    double = [jnp.zeros((RHS, BLOCK), f32)] * 4
    for step, (i, j) in enumerate(PAIRED):
        double[i] += times(rounded[j], tiles[4 + step])
    for i in range(4):
        partial[i] = own_noise[i] * image[i] * 256.0 + single[i] + 2.0 * double[i]


def upward(upper, tiles, before, partial):
    double = [jnp.zeros((RHS, BLOCK), f32)] * 4
    for step in range(16):
        double[step % 4] += times(upper[step // 4], tiles[step])
    for i in range(4):
        partial[i] = before[i] + 2.0 * double[i]


def cross_tile(step, tiles_early, tiles_late):
    first = len(CROSS) - len(LATE)
    return tiles_early[10 + step] if step < first else tiles_late[step - first]


def by_column(from_column, tiles_early, tiles_late, tiles_up, before, partial, raised):
    border = {4: from_column[0], 5: from_column[1]}
    single = [jnp.zeros((RHS, BLOCK), f32)] * 4
    lifted = [jnp.zeros((RHS, BLOCK), f32)] * 4
    for step, (i, j) in enumerate(CROSS):
        if j in border:
            single[i] += times(border[j], cross_tile(step, tiles_early, tiles_late))
            lifted[i] += times(border[j], tiles_up[16 + step])
    for i in range(4):
        partial[i] = before[i] + single[i]
        raised[i] = lifted[i]


def outside(from_row, from_corner, upper, tiles_early, tiles_late, tiles_up, before, lifted, image, products, copies):
    border = {6: from_row[0], 7: from_row[1], 8: from_corner[0]}
    single = [jnp.zeros((RHS, BLOCK), f32)] * 4
    raised = [lifted[i] for i in range(4)]
    for step, (i, j) in enumerate(CROSS):
        if j in border:
            single[i] += times(border[j], cross_tile(step, tiles_early, tiles_late))
            raised[i] += times(border[j], tiles_up[16 + step])
    third = gram(
        side_by_side([image[i] for i in range(4)] + [upper[i].astype(f32) for i in range(4)]),
        side_by_side([before[i] + single[i] for i in range(4)] + [2.0 * raised[i] for i in range(4)]),
    ) * (1.0 / 256.0)
    known = products[...]
    ordered = jnp.concatenate(
        [known[16:32, 16:32], known[16:32, 0:16], known[0:16, 0:16], third], axis=1
    )
    packed = jnp.concatenate([ordered[0:8], ordered[8:16]], axis=1)
    copies[...] = jnp.broadcast_to(packed[None], copies.shape)


def add_up(arrived, copies):
    copies[...] = jnp.broadcast_to(jnp.sum(arrived[...], axis=0, keepdims=True), copies.shape)


def inverse_of_two(block):
    (a, b), (c, d) = block
    scale = 1.0 / (a * d - b * c)
    return ((d * scale, -b * scale), (-c * scale, a * scale))


def product_of_two(first, second):
    return tuple(
        tuple(first[p][0] * second[0][q] + first[p][1] * second[1][q] for q in range(2))
        for p in range(2)
    )


def eliminate_four(value, rows, k):
    columns = [jnp.broadcast_to(value[:, k + q:k + q + 1], value.shape) for q in range(4)]
    lines = [value[k + q:k + q + 1] for q in range(4)]
    pivot = [[columns[q][k + p:k + p + 1] for q in range(4)] for p in range(4)]

    def block(p, q):
        return ((pivot[p][q], pivot[p][q + 1]), (pivot[p + 1][q], pivot[p + 1][q + 1]))

    head = inverse_of_two(block(0, 0))
    right = block(0, 2)
    reduced = product_of_two(block(2, 0), head)
    corner = block(2, 2)
    taken = product_of_two(reduced, right)
    tail = inverse_of_two(
        tuple(tuple(corner[p][q] - taken[p][q] for q in range(2)) for p in range(2))
    )
    low = [lines[2 + p] - (reduced[p][0] * lines[0] + reduced[p][1] * lines[1]) for p in range(2)]
    low = [tail[p][0] * low[0] + tail[p][1] * low[1] for p in range(2)]
    high = [lines[p] - (right[p][0] * low[0] + right[p][1] * low[1]) for p in range(2)]
    high = [head[p][0] * high[0] + head[p][1] * high[1] for p in range(2)]
    new = high + low
    value = (value - columns[0] * new[0] - columns[1] * new[1]) - (
        columns[2] * new[2] + columns[3] * new[3]
    )
    for q in range(4):
        value = jnp.where(rows == k + q, new[q], value)
    return value


def conclude(arrived, own_sides, image, result):
    packed = jnp.sum(arrived[...], axis=0)
    ordered = jnp.concatenate([packed[:, 0:64], packed[:, 64:128]], axis=0)
    start, first, second, third = (ordered[:, 16 * part:16 * part + 16] for part in range(4))
    square = jnp.concatenate(
        [jnp.concatenate([first, second], axis=1), jnp.concatenate([second, third], axis=1)], axis=0
    )
    square = jnp.concatenate([square, jnp.zeros((32, 96), f32)], axis=1)
    flipped = jnp.transpose(jnp.concatenate([square, jnp.zeros((96, 128), f32)], axis=0))[0:32]
    square = 0.5 * (square + flipped)
    known = jnp.concatenate([start, square[0:16, 0:16]], axis=0)
    value = jnp.concatenate([square[:, 0:32], known, jnp.zeros((32, 80), f32)], axis=1)
    rows = lax.broadcasted_iota(jnp.int32, (32, 128), 0)
    for k in range(0, 32, 4):
        value = eliminate_four(value, rows, k)
    weights = jnp.transpose(jnp.concatenate([value, jnp.zeros((96, 128), f32)], axis=0))[32:48, 0:32]
    member = lax.axis_index("sub")
    for i, (row, column) in enumerate(OWN):
        both = jnp.concatenate([own_sides[i], image[i]], axis=0)
        place = (row ^ (member & 1)) + 2 * (column ^ (member >> 1))
        result[place] = jnp.dot(
            weights, both, precision=lax.Precision.HIGHEST, preferred_element_type=f32
        )


def local(regions, members, points, noise_var, right_sides, pair_list, pair_count):
    everyone = regions * members

    def from_region(value, step):
        pairs = [
            (source, source - step)
            for source in range(regions)
            if 0 <= source - step < regions
        ]
        return lax.ppermute(value, "region", pairs)

    def from_member(value, mask):
        return lax.ppermute(value, "sub", [(source, source ^ mask) for source in range(members)])

    def swap(copies, stride):
        size = copies.shape[0]
        groups = [
            [first + stride * place for place in range(size)]
            for first in range(everyone)
            if first // stride % size == 0
        ]
        return lax.all_to_all(
            copies, ("region", "sub"), 0, 0, axis_index_groups=groups, tiled=True
        )

    def shape(*dims, dtype=f32):
        return jax.ShapeDtypeStruct(dims, dtype)

    def held(*dims, dtype=bf16):
        return pltpu.VMEM(dims, dtype)

    tile_flops = 2 * BLOCK * BLOCK * 256
    field = (4, RHS, BLOCK)
    buffers = [pltpu.VMEM((BLOCK, BLOCK), f32)] * 2
    sent, left, right, own_sides, own_noise = call(
        prepare, "prepare",
        (shape(9, 32, BLOCK, dtype=bf16), shape(9, BLOCK, FEATURES, dtype=bf16),
         shape(4, FEATURES, BLOCK, dtype=bf16), shape(*field), shape(4, 1, BLOCK)),
        [pltpu.with_memory_space_constraint(value, pltpu.HBM) for value in (points, noise_var, right_sides)],
        tile_flops,
        [pltpu.VMEM(value.shape, f32) for value in (points, noise_var, right_sides)]
        + [pltpu.SemaphoreType.DMA((3,))],
        pltpu.HBM,
    )
    above = from_region(sent, 1)
    totals, tiles_early = call(
        within_layer, "within_layer", (shape(*field), held(len(EARLY), BLOCK, BLOCK)),
        (sent, left, right), len(EARLY) * 4 * tile_flops, buffers,
    )
    totals, passed, tiles_up = call(
        above_own, "above_own",
        (shape(*field), shape(*field, dtype=bf16), held(25, BLOCK, BLOCK)),
        (sent, left, right, above, totals), 25 * 4 * tile_flops,
        [pltpu.VMEM((4, BLOCK, FEATURES), bf16), pltpu.VMEM((4, FEATURES, BLOCK), bf16),
         pltpu.VMEM(field, f32)] + buffers,
    )
    arrived = from_region(passed, -1)
    totals, tiles_late = call(
        borders, "borders", (shape(*field), held(len(LATE), BLOCK, BLOCK)),
        (sent, left, right, above, totals), 16 * 4 * tile_flops,
        [pltpu.VMEM((5, BLOCK, FEATURES), bf16)] + buffers,
    )
    image, rounded = call(
        finish_image, "finish_image", (shape(*field), shape(*field, dtype=bf16)),
        (totals, arrived, own_noise, own_sides), tile_flops // 8,
    )
    upper = from_region(rounded, 1)
    from_row = from_member(rounded[2:4], 1)
    from_column = from_member(rounded[1::2], 2)
    from_corner = from_member(rounded[3:4], 3)
    products, partial = call(
        inside, "inside", (shape(32, 32), shape(*field)),
        (own_sides, image, rounded, own_noise, tiles_early), 10 * 2 * tile_flops,
    )
    partial = call(
        upward, "upward", shape(*field), (upper, tiles_up, partial), 16 * 2 * tile_flops,
    )
    partial, raised = call(
        by_column, "by_column", (shape(*field), shape(*field)),
        (from_column, tiles_early, tiles_late, tiles_up, partial), 8 * 2 * tile_flops,
    )
    plane = 8 * members
    copies = call(
        outside, "outside", shape(plane, 8, 128),
        (from_row, from_corner, upper, tiles_early, tiles_late, tiles_up, partial, raised, image,
         products),
        10 * 2 * tile_flops,
    )
    arrived = swap(copies, 1)
    copies = call(add_up, "add_up", shape(everyone // plane, 8, 128), (arrived,), 1024)
    arrived = swap(copies, plane)
    return call(
        conclude, "conclude", shape(*field), (arrived, own_sides, image), tile_flops,
    )


def solution(mesh):
    return jax.shard_map(
        functools.partial(local, mesh.shape["region"], mesh.shape["sub"]),
        mesh=mesh,
        in_specs=(
            P(None, "region", None),
            P("region", None),
            P("region", None, None),
            P("region", "sub", None, None),
            P("region", "sub"),
        ),
        out_specs=P(("region", "sub"), None, None),
        check_vma=False,
    )
```

```python
import functools
import jax
import jax.numpy as jnp
from jax import lax
from jax.experimental import pallas as pl
from jax.experimental.pallas import tpu as pltpu
from jax.sharding import PartitionSpec as P

OWN = ((0, 0), (0, 1), (1, 0), (1, 1))
BORDER = ((0, 2), (1, 2), (2, 0), (2, 1), (2, 2))
WINDOW = OWN + BORDER
PAIRED = tuple((i, j) for j in range(4) for i in range(j))
CROSS = tuple(
    (i, j)
    for j in range(4, 9)
    for i in range(4)
    if max(abs(OWN[i][0] - WINDOW[j][0]), abs(OWN[i][1] - WINDOW[j][1])) <= 1
)
HALF = 256
PACKED = 3
EARLY = PAIRED + CROSS[:6]
LATE = CROSS[6:]
BLOCK = 512
RHS = 16
FEATURES = 64
f32, bf16 = jnp.float32, jnp.bfloat16
VMEM = pl.BlockSpec(memory_space=pltpu.VMEM)


def call(kernel, name, out_shape, args, flops, scratch=(), args_space=pltpu.VMEM):
    return pl.pallas_call(
        kernel,
        name=name,
        out_shape=out_shape,
        in_specs=[pl.BlockSpec(memory_space=args_space)] * len(args),
        out_specs=jax.tree.map(lambda _: VMEM, out_shape),
        scratch_shapes=scratch,
        compiler_params=pltpu.CompilerParams(vmem_limit_bytes=16 << 20),
        cost_estimate=pl.CostEstimate(flops=flops, bytes_accessed=1 << 20, transcendentals=0),
    )(*args)


def split(value):
    high = value.astype(bf16).astype(f32)
    rest = value - high
    middle = rest.astype(bf16).astype(f32)
    return high, middle, rest - middle


def feature_rows(place):
    rows = lax.broadcasted_iota(jnp.int32, place.shape, 0)
    parts = split(place)
    norms = split(16.0 * jnp.sum(place * place, axis=0, keepdims=True))
    left, right = [], []
    for group, (a, b) in enumerate(((0, 0), (0, 1), (1, 0), (1, 1), (0, 2), (2, 0), (1, 2), (2, 1))):
        one_left, one_right = -32.0 * parts[a], parts[b]
        if group < 3:
            norm = jnp.broadcast_to(norms[group], place.shape)
            one_left = jnp.where(rows == 3, norm, jnp.where(rows == 4, 1.0, one_left))
            one_right = jnp.where(rows == 4, norm, jnp.where(rows == 3, 1.0, one_right))
        left.append(one_left)
        right.append(one_right)
    return jnp.concatenate(left, axis=0), jnp.concatenate(right, axis=0)


def prepare(
    points_far, noise_far, sides_far, sent, left, right, own_sides, own_noise,
    points, noise_var, right_sides, arrivals,
):
    copies = [
        pltpu.make_async_copy(source, target, arrivals.at[place])
        for place, (source, target) in enumerate(
            ((points_far, points), (noise_far, noise_var), (sides_far, right_sides))
        )
    ]
    for copy in copies:
        copy.start()
    copies[0].wait()
    region = lax.axis_index("region")
    member = lax.axis_index("sub")
    row_half, column_half = member & 1, member >> 1
    rows = lax.broadcasted_iota(jnp.int32, (8, BLOCK), 0)
    centers = (
        region.astype(f32) + 0.5,
        row_half.astype(f32) + 1.5,
        column_half.astype(f32) + 1.5,
    )
    blocks = []
    for index, (row, column) in enumerate(WINDOW):
        row = jnp.where(row_half == 1, 3 - row, row)
        column = jnp.where(column_half == 1, 3 - column, column)
        block = (row & 1) + 2 * (column & 1) + 4 * (row >> 1) + 8 * (column >> 1)
        place = jnp.zeros((8, BLOCK), f32)
        for axis in range(3):
            line = points[axis, pl.ds(block, 1), :] - centers[axis]
            place = jnp.where(rows == axis, jnp.broadcast_to(line, place.shape), place)
        blocks.append(block)
        high, middle, low = split(place)
        sent[index, 16:32, :] = jnp.concatenate(
            [high + pltpu.roll(low, 3, 0), middle], axis=0
        ).astype(bf16)
        left_rows, right_rows = feature_rows(place)
        left[index] = jnp.transpose(left_rows).astype(bf16)
        if index < 4:
            right[index] = right_rows.astype(bf16)
    copies[1].wait()
    copies[2].wait()
    for index, block in enumerate(blocks):
        side = right_sides[block]
        sent[index, 0:16, :] = side.astype(bf16)
        if index < 4:
            own_sides[index] = side
            own_noise[index] = noise_var[pl.ds(block, 1), :]


def neighbour_features(packed, shift):
    rows = lax.broadcasted_iota(jnp.int32, (8, BLOCK), 0)
    packed = packed.astype(f32)
    top, middle = packed[0:8], packed[8:16]
    place = jnp.where(rows < 3, top + middle + pltpu.roll(top, 5, 0), 0.0)
    place = jnp.where(rows == 0, place + shift, place)
    return feature_rows(place)


def sweep(lefts, rights, buffers, use, fills=()):
    count = len(fills) + len(lefts)

    def distances(step):
        buffer = buffers[step % 2]
        if step < len(fills):
            fills[step](buffer)
        else:
            place = step - len(fills)
            buffer[...] = jnp.dot(lefts[place](), rights[place](), preferred_element_type=f32)

    distances(0)
    for step in range(count):
        if step + 1 < count:
            distances(step + 1)
        parts = []
        for start in range(0, BLOCK, 64):
            squared = jnp.maximum(buffers[step % 2][start:start + 64, :], 1e-30)
            falloff = jnp.maximum(4.0 - squared * lax.rsqrt(squared), 0.0)
            second = falloff * falloff
            parts.append(((second * second) * (5.0 - falloff)).astype(bf16))
        use(step, jnp.concatenate(parts, axis=0))


def times(vectors, tile):
    return jnp.dot(vectors, tile, preferred_element_type=f32)


def times_transposed(vectors, tile):
    return lax.dot_general(vectors, tile, (((1,), (1,)), ((), ())), preferred_element_type=f32)


def within_layer(sent, left, right, totals, tiles, *buffers):
    totals[...] = jnp.zeros_like(totals)

    def upper_halves(first, buffer):
        for place in range(2):
            i = first + place
            buffer[place * HALF:(place + 1) * HALF, :] = jnp.dot(
                left[i, 0:HALF, :], right[i], preferred_element_type=f32
            )

    def last_quarters(buffer):
        for i in range(4):
            down, along = i // 2 * HALF, i % 2 * HALF
            buffer[down:down + HALF, along:along + HALF] = jnp.dot(
                left[i, HALF:BLOCK, :], right[i, :, HALF:BLOCK], preferred_element_type=f32
            )

    def use(step, tile):
        tiles[step] = tile
        if step < 2:
            for place in range(2):
                i = 2 * step + place
                part = tile[place * HALF:(place + 1) * HALF, :]
                totals[i] += times(sent[i, 0:16, 0:HALF], part)
                totals[i, :, 0:HALF] += times_transposed(sent[i, 0:16, HALF:BLOCK], part[:, HALF:BLOCK])
        elif step == 2:
            for i in range(4):
                down, along = i // 2 * HALF, i % 2 * HALF
                part = tile[down:down + HALF, along:along + HALF]
                totals[i, :, HALF:BLOCK] += times(sent[i, 0:16, HALF:BLOCK], part)
        else:
            i, j = EARLY[step - PACKED]
            totals[i] += times(sent[j, 0:16, :], tile)
            if j < 4:
                totals[j] += times_transposed(sent[i, 0:16, :], tile)

    sweep(
        [lambda j=j: left[j] for i, j in EARLY],
        [lambda i=i: right[i] for i, j in EARLY],
        buffers, use,
        [functools.partial(upper_halves, 0), functools.partial(upper_halves, 2), last_quarters],
    )


def above_own(
    sent, left, right, above, before, totals, leaving, tiles,
    left_above, right_above, passed, *buffers,
):
    totals[...] = before[...]
    passed[...] = jnp.zeros_like(passed)
    for j in range(4):
        left_rows, right_rows = neighbour_features(above[j, 16:32, :], 1.0)
        left_above[j] = jnp.transpose(left_rows).astype(bf16)
        right_above[j] = right_rows.astype(bf16)

    def use(step, tile):
        tiles[step] = tile
        if step < 16:
            i, j = step % 4, step // 4
            totals[i] += times(above[j, 0:16, :], tile)
            passed[j] += times_transposed(sent[i, 0:16, :], tile)
        else:
            j, border = CROSS[step - 16]
            passed[j] += times(sent[border, 0:16, :], tile)

    sweep(
        [lambda j=step // 4: left_above[j] for step in range(16)]
        + [lambda border=border: left[border] for j, border in CROSS],
        [lambda i=step % 4: right[i] for step in range(16)]
        + [lambda j=j: right_above[j] for j, border in CROSS],
        buffers, use,
    )
    leaving[...] = passed[...].astype(bf16)


def borders(sent, left, right, above, before, totals, tiles, left_above, *buffers):
    totals[...] = before[...]
    for j in range(5):
        left_above[j] = jnp.transpose(
            neighbour_features(above[4 + j, 16:32, :], 1.0)[0]
        ).astype(bf16)

    def use(step, tile):
        if step < len(LATE):
            i, j = LATE[step]
            tiles[step] = tile
            totals[i] += times(sent[j, 0:16, :], tile)
        else:
            i, j = CROSS[step - len(LATE)]
            totals[i] += times(above[j, 0:16, :], tile)

    sweep(
        [lambda j=j: left[j] for i, j in LATE] + [lambda j=j: left_above[j - 4] for i, j in CROSS],
        [lambda i=i: right[i] for i, j in LATE + CROSS],
        buffers, use,
    )


def finish_image(totals, arrived, own_noise, own_sides, image, rounded):
    value = (totals[...] + arrived[...].astype(f32)) * (1.0 / 256.0) + own_noise[...] * own_sides[...]
    image[...] = value
    rounded[...] = value.astype(bf16)


def gram(first, second):
    return lax.dot_general(
        first, second, (((1,), (1,)), ((), ())),
        precision=lax.Precision.HIGHEST, preferred_element_type=f32,
    )


def side_by_side(blocks):
    return jnp.concatenate(blocks, axis=1)


def inside(own_sides, image, rounded, own_noise, tiles, products, partial):
    both = jnp.concatenate(
        [side_by_side([image[i] for i in range(4)]), side_by_side([own_sides[i] for i in range(4)])],
        axis=0,
    )
    products[...] = gram(both, both)
    double = [jnp.zeros((RHS, BLOCK), f32)] * 4
    for step, (i, j) in enumerate(PAIRED):
        double[i] += times(rounded[j], tiles[PACKED + step])
    for i in range(4):
        start = i % 2 * HALF
        upper = times(rounded[i, :, 0:HALF], tiles[i // 2, start:start + HALF, :])
        down = i // 2 * HALF
        last = times(rounded[i, :, HALF:BLOCK], tiles[2, down:down + HALF, start:start + HALF])
        single = jnp.concatenate([upper[:, 0:HALF], 2.0 * upper[:, HALF:BLOCK] + last], axis=1)
        partial[i] = own_noise[i] * image[i] * 256.0 + single + 2.0 * double[i]


def upward(upper, tiles, before, partial):
    double = [jnp.zeros((RHS, BLOCK), f32)] * 4
    for step in range(16):
        double[step % 4] += times(upper[step // 4], tiles[step])
    for i in range(4):
        partial[i] = before[i] + 2.0 * double[i]


def cross_products(border, tiles_early, tiles_late, tiles_up, single, raised):
    first = len(CROSS) - len(LATE)
    for step, (i, j) in enumerate(CROSS):
        if j in border:
            tile = tiles_early[PACKED + 6 + step] if step < first else tiles_late[step - first]
            single[i] += times(border[j], tile)
            raised[i] += times(border[j], tiles_up[16 + step])


def by_row(from_row, from_corner, upper, tiles_early, tiles_late, tiles_up, before, image, third):
    border = {6: from_row[0], 7: from_row[1], 8: from_corner[0]}
    single = [before[i] for i in range(4)]
    raised = [jnp.zeros((RHS, BLOCK), f32)] * 4
    cross_products(border, tiles_early, tiles_late, tiles_up, single, raised)
    third[...] = gram(
        side_by_side([image[i] for i in range(4)] + [upper[i].astype(f32) for i in range(4)]),
        side_by_side(single + [2.0 * raised[i] for i in range(4)]),
    )


def by_column(from_column, upper, tiles_early, tiles_late, tiles_up, so_far, image, products, copies):
    border = {4: from_column[0], 5: from_column[1]}
    single = [jnp.zeros((RHS, BLOCK), f32)] * 4
    raised = [jnp.zeros((RHS, BLOCK), f32)] * 4
    cross_products(border, tiles_early, tiles_late, tiles_up, single, raised)
    third = (so_far[...] + gram(
        side_by_side([image[i] for i in (1, 3)] + [upper[i].astype(f32) for i in (1, 3)]),
        side_by_side([single[i] for i in (1, 3)] + [2.0 * raised[i] for i in (1, 3)]),
    )) * (1.0 / 256.0)
    known = products[...]
    ordered = jnp.concatenate(
        [known[16:32, 16:32], known[16:32, 0:16], known[0:16, 0:16], third], axis=1
    )
    packed = jnp.concatenate([ordered[0:8], ordered[8:16]], axis=1)
    copies[...] = jnp.broadcast_to(packed[None], copies.shape)


def add_up(arrived, copies):
    copies[...] = jnp.broadcast_to(jnp.sum(arrived[...], axis=0, keepdims=True), copies.shape)


def inverse_of_two(block):
    (a, b), (c, d) = block
    scale = 1.0 / (a * d - b * c)
    return ((d * scale, -b * scale), (-c * scale, a * scale))


def product_of_two(first, second):
    return tuple(
        tuple(first[p][0] * second[0][q] + first[p][1] * second[1][q] for q in range(2))
        for p in range(2)
    )


def eliminate_four(value, rows, k):
    columns = [jnp.broadcast_to(value[:, k + q:k + q + 1], value.shape) for q in range(4)]
    lines = [value[k + q:k + q + 1] for q in range(4)]
    pivot = [[columns[q][k + p:k + p + 1] for q in range(4)] for p in range(4)]

    def block(p, q):
        return ((pivot[p][q], pivot[p][q + 1]), (pivot[p + 1][q], pivot[p + 1][q + 1]))

    head = inverse_of_two(block(0, 0))
    right = block(0, 2)
    reduced = product_of_two(block(2, 0), head)
    corner = block(2, 2)
    taken = product_of_two(reduced, right)
    tail = inverse_of_two(
        tuple(tuple(corner[p][q] - taken[p][q] for q in range(2)) for p in range(2))
    )
    low = [lines[2 + p] - (reduced[p][0] * lines[0] + reduced[p][1] * lines[1]) for p in range(2)]
    low = [tail[p][0] * low[0] + tail[p][1] * low[1] for p in range(2)]
    high = [lines[p] - (right[p][0] * low[0] + right[p][1] * low[1]) for p in range(2)]
    high = [head[p][0] * high[0] + head[p][1] * high[1] for p in range(2)]
    new = high + low
    value = (value - columns[0] * new[0] - columns[1] * new[1]) - (
        columns[2] * new[2] + columns[3] * new[3]
    )
    for q in range(4):
        value = jnp.where(rows == k + q, new[q], value)
    return value


def conclude(arrived, own_sides, image, result):
    packed = jnp.sum(arrived[...], axis=0)
    ordered = jnp.concatenate([packed[:, 0:64], packed[:, 64:128]], axis=0)
    start, first, second, third = (ordered[:, 16 * part:16 * part + 16] for part in range(4))
    square = jnp.concatenate(
        [jnp.concatenate([first, second], axis=1), jnp.concatenate([second, third], axis=1)], axis=0
    )
    square = jnp.concatenate([square, jnp.zeros((32, 96), f32)], axis=1)
    flipped = jnp.transpose(jnp.concatenate([square, jnp.zeros((96, 128), f32)], axis=0))[0:32]
    square = 0.5 * (square + flipped)
    known = jnp.concatenate([start, square[0:16, 0:16]], axis=0)
    value = jnp.concatenate([square[:, 0:32], known, jnp.zeros((32, 80), f32)], axis=1)
    rows = lax.broadcasted_iota(jnp.int32, (32, 128), 0)
    for k in range(0, 32, 4):
        value = eliminate_four(value, rows, k)
    weights = jnp.transpose(jnp.concatenate([value, jnp.zeros((96, 128), f32)], axis=0))[32:48, 0:32]
    member = lax.axis_index("sub")
    for i, (row, column) in enumerate(OWN):
        both = jnp.concatenate([own_sides[i], image[i]], axis=0)
        place = (row ^ (member & 1)) + 2 * (column ^ (member >> 1))
        result[place] = jnp.dot(
            weights, both, precision=lax.Precision.HIGHEST, preferred_element_type=f32
        )


def local(regions, members, points, noise_var, right_sides, pair_list, pair_count):
    everyone = regions * members

    def from_region(value, step):
        pairs = [
            (source, source - step)
            for source in range(regions)
            if 0 <= source - step < regions
        ]
        return lax.ppermute(value, "region", pairs)

    def from_member(value, mask):
        return lax.ppermute(value, "sub", [(source, source ^ mask) for source in range(members)])

    def swap(copies, stride):
        size = copies.shape[0]
        groups = [
            [first + stride * place for place in range(size)]
            for first in range(everyone)
            if first // stride % size == 0
        ]
        return lax.all_to_all(
            copies, ("region", "sub"), 0, 0, axis_index_groups=groups, tiled=True
        )

    def shape(*dims, dtype=f32):
        return jax.ShapeDtypeStruct(dims, dtype)

    def held(*dims, dtype=bf16):
        return pltpu.VMEM(dims, dtype)

    tile_flops = 2 * BLOCK * BLOCK * 256
    field = (4, RHS, BLOCK)
    buffers = [pltpu.VMEM((BLOCK, BLOCK), f32)] * 2
    sent, left, right, own_sides, own_noise = call(
        prepare, "prepare",
        (shape(9, 32, BLOCK, dtype=bf16), shape(9, BLOCK, FEATURES, dtype=bf16),
         shape(4, FEATURES, BLOCK, dtype=bf16), shape(*field), shape(4, 1, BLOCK)),
        [pltpu.with_memory_space_constraint(value, pltpu.HBM) for value in (points, noise_var, right_sides)],
        tile_flops,
        [pltpu.VMEM(value.shape, f32) for value in (points, noise_var, right_sides)]
        + [pltpu.SemaphoreType.DMA((3,))],
        pltpu.HBM,
    )
    above = from_region(sent, 1)
    totals, tiles_early = call(
        within_layer, "within_layer", (shape(*field), held(PACKED + len(EARLY), BLOCK, BLOCK)),
        (sent, left, right), (PACKED + len(EARLY)) * 4 * tile_flops, buffers,
    )
    totals, passed, tiles_up = call(
        above_own, "above_own",
        (shape(*field), shape(*field, dtype=bf16), held(25, BLOCK, BLOCK)),
        (sent, left, right, above, totals), 25 * 4 * tile_flops,
        [pltpu.VMEM((4, BLOCK, FEATURES), bf16), pltpu.VMEM((4, FEATURES, BLOCK), bf16),
         pltpu.VMEM(field, f32)] + buffers,
    )
    arrived = from_region(passed, -1)
    totals, tiles_late = call(
        borders, "borders", (shape(*field), held(len(LATE), BLOCK, BLOCK)),
        (sent, left, right, above, totals), 16 * 4 * tile_flops,
        [pltpu.VMEM((5, BLOCK, FEATURES), bf16)] + buffers,
    )
    image, rounded = call(
        finish_image, "finish_image", (shape(*field), shape(*field, dtype=bf16)),
        (totals, arrived, own_noise, own_sides), tile_flops // 8,
    )
    upper = from_region(rounded, 1)
    from_row = from_member(rounded[2:4], 1)
    from_column = from_member(rounded[1::2], 2)
    from_corner = from_member(rounded[3:4], 3)
    products, partial = call(
        inside, "inside", (shape(32, 32), shape(*field)),
        (own_sides, image, rounded, own_noise, tiles_early), 10 * 2 * tile_flops,
    )
    partial = call(
        upward, "upward", shape(*field), (upper, tiles_up, partial), 16 * 2 * tile_flops,
    )
    third = call(
        by_row, "by_row", shape(RHS, RHS),
        (from_row, from_corner, upper, tiles_early, tiles_late, tiles_up, partial, image),
        10 * 2 * tile_flops,
    )
    plane = 8 * members
    copies = call(
        by_column, "by_column", shape(plane, 8, 128),
        (from_column, upper, tiles_early, tiles_late, tiles_up, third, image, products),
        8 * 2 * tile_flops,
    )
    arrived = swap(copies, 1)
    copies = call(add_up, "add_up", shape(everyone // plane, 8, 128), (arrived,), 1024)
    arrived = swap(copies, plane)
    return call(
        conclude, "conclude", shape(*field), (arrived, own_sides, image), tile_flops,
    )


def solution(mesh):
    return jax.shard_map(
        functools.partial(local, mesh.shape["region"], mesh.shape["sub"]),
        mesh=mesh,
        in_specs=(
            P(None, "region", None),
            P("region", None),
            P("region", None, None),
            P("region", "sub", None, None),
            P("region", "sub"),
        ),
        out_specs=P(("region", "sub"), None, None),
        check_vma=False,
    )
```

```python
import functools
import jax
import jax.numpy as jnp
from jax import lax
from jax.experimental import pallas as pl
from jax.experimental.pallas import tpu as pltpu
from jax.sharding import PartitionSpec as P

OWN = ((0, 0), (0, 1), (1, 0), (1, 1))
BORDER = ((0, 2), (1, 2), (2, 0), (2, 1), (2, 2))
WINDOW = OWN + BORDER
PAIRED = tuple((i, j) for j in range(4) for i in range(j))
CROSS = tuple(
    (i, j)
    for j in range(4, 9)
    for i in range(4)
    if max(abs(OWN[i][0] - WINDOW[j][0]), abs(OWN[i][1] - WINDOW[j][1])) <= 1
)
HALF = 256
PACKED = 3
EARLY = PAIRED + CROSS[:6]
LATE = CROSS[6:]
BLOCK = 512
RHS = 16
FEATURES = 64
f32, bf16 = jnp.float32, jnp.bfloat16
VMEM = pl.BlockSpec(memory_space=pltpu.VMEM)


def call(kernel, name, out_shape, args, flops, scratch=(), args_space=pltpu.VMEM):
    return pl.pallas_call(
        kernel,
        name=name,
        out_shape=out_shape,
        in_specs=[pl.BlockSpec(memory_space=args_space)] * len(args),
        out_specs=jax.tree.map(lambda _: VMEM, out_shape),
        scratch_shapes=scratch,
        compiler_params=pltpu.CompilerParams(vmem_limit_bytes=16 << 20),
        cost_estimate=pl.CostEstimate(flops=flops, bytes_accessed=1 << 20, transcendentals=0),
    )(*args)


def split(value):
    high = value.astype(bf16).astype(f32)
    rest = value - high
    middle = rest.astype(bf16).astype(f32)
    return high, middle, rest - middle


def feature_rows(place):
    rows = lax.broadcasted_iota(jnp.int32, place.shape, 0)
    parts = split(place)
    norms = split(16.0 * jnp.sum(place * place, axis=0, keepdims=True))
    left, right = [], []
    for group, (a, b) in enumerate(((0, 0), (0, 1), (1, 0), (1, 1), (0, 2), (2, 0), (1, 2), (2, 1))):
        one_left, one_right = -32.0 * parts[a], parts[b]
        if group < 3:
            norm = jnp.broadcast_to(norms[group], place.shape)
            one_left = jnp.where(rows == 3, norm, jnp.where(rows == 4, 1.0, one_left))
            one_right = jnp.where(rows == 4, norm, jnp.where(rows == 3, 1.0, one_right))
        left.append(one_left)
        right.append(one_right)
    return jnp.concatenate(left, axis=0), jnp.concatenate(right, axis=0)


def prepare(
    points_far, noise_far, sides_far, sent, left, right, own_sides, own_noise,
    points, noise_var, right_sides, arrivals,
):
    copies = [
        pltpu.make_async_copy(source, target, arrivals.at[place])
        for place, (source, target) in enumerate(
            ((points_far, points), (noise_far, noise_var), (sides_far, right_sides))
        )
    ]
    for copy in copies:
        copy.start()
    copies[0].wait()
    region = lax.axis_index("region")
    member = lax.axis_index("sub")
    row_half, column_half = member & 1, member >> 1
    rows = lax.broadcasted_iota(jnp.int32, (8, BLOCK), 0)
    centers = (
        region.astype(f32) + 0.5,
        row_half.astype(f32) + 1.5,
        column_half.astype(f32) + 1.5,
    )
    blocks = []
    for index, (row, column) in enumerate(WINDOW):
        row = jnp.where(row_half == 1, 3 - row, row)
        column = jnp.where(column_half == 1, 3 - column, column)
        block = (row & 1) + 2 * (column & 1) + 4 * (row >> 1) + 8 * (column >> 1)
        place = jnp.zeros((8, BLOCK), f32)
        for axis in range(3):
            line = points[axis, pl.ds(block, 1), :] - centers[axis]
            place = jnp.where(rows == axis, jnp.broadcast_to(line, place.shape), place)
        blocks.append(block)
        high, middle, low = split(place)
        sent[index, 16:32, :] = jnp.concatenate(
            [high + pltpu.roll(low, 3, 0), middle], axis=0
        ).astype(bf16)
        left_rows, right_rows = feature_rows(place)
        left[index] = jnp.transpose(left_rows).astype(bf16)
        if index < 4:
            right[index] = right_rows.astype(bf16)
    copies[1].wait()
    copies[2].wait()
    for index, block in enumerate(blocks):
        side = right_sides[block]
        sent[index, 0:16, :] = side.astype(bf16)
        if index < 4:
            own_sides[index] = side
            own_noise[index] = noise_var[pl.ds(block, 1), :]


def neighbour_features(packed, shift):
    rows = lax.broadcasted_iota(jnp.int32, (8, BLOCK), 0)
    packed = packed.astype(f32)
    top, middle = packed[0:8], packed[8:16]
    place = jnp.where(rows < 3, top + middle + pltpu.roll(top, 5, 0), 0.0)
    place = jnp.where(rows == 0, place + shift, place)
    return feature_rows(place)


def sweep(lefts, rights, buffers, use, fills=()):
    count = len(fills) + len(lefts)

    def distances(step):
        buffer = buffers[step % 2]
        if step < len(fills):
            fills[step](buffer)
        else:
            place = step - len(fills)
            buffer[...] = jnp.dot(lefts[place](), rights[place](), preferred_element_type=f32)

    distances(0)
    for step in range(count):
        if step + 1 < count:
            distances(step + 1)
        parts = []
        for start in range(0, BLOCK, 64):
            squared = jnp.maximum(buffers[step % 2][start:start + 64, :], 1e-30)
            falloff = jnp.maximum(4.0 - squared * lax.rsqrt(squared), 0.0)
            second = falloff * falloff
            parts.append(((second * second) * (5.0 - falloff)).astype(bf16))
        use(step, jnp.concatenate(parts, axis=0))


def times(vectors, tile):
    return jnp.dot(vectors, tile, preferred_element_type=f32)


def times_transposed(vectors, tile):
    return lax.dot_general(vectors, tile, (((1,), (1,)), ((), ())), preferred_element_type=f32)


def within_layer(sent, left, right, totals, tiles, *buffers):
    totals[...] = jnp.zeros_like(totals)

    def upper_halves(first, buffer):
        for place in range(2):
            i = first + place
            buffer[place * HALF:(place + 1) * HALF, :] = jnp.dot(
                left[i, 0:HALF, :], right[i], preferred_element_type=f32
            )

    def last_quarters(buffer):
        for i in range(4):
            down, along = i // 2 * HALF, i % 2 * HALF
            buffer[down:down + HALF, along:along + HALF] = jnp.dot(
                left[i, HALF:BLOCK, :], right[i, :, HALF:BLOCK], preferred_element_type=f32
            )

    def use(step, tile):
        tiles[step] = tile
        if step < 2:
            for place in range(2):
                i = 2 * step + place
                part = tile[place * HALF:(place + 1) * HALF, :]
                totals[i] += times(sent[i, 0:16, 0:HALF], part)
                totals[i, :, 0:HALF] += times_transposed(sent[i, 0:16, HALF:BLOCK], part[:, HALF:BLOCK])
        elif step == 2:
            for i in range(4):
                down, along = i // 2 * HALF, i % 2 * HALF
                part = tile[down:down + HALF, along:along + HALF]
                totals[i, :, HALF:BLOCK] += times(sent[i, 0:16, HALF:BLOCK], part)
        else:
            i, j = EARLY[step - PACKED]
            totals[i] += times(sent[j, 0:16, :], tile)
            if j < 4:
                totals[j] += times_transposed(sent[i, 0:16, :], tile)

    sweep(
        [lambda j=j: left[j] for i, j in EARLY],
        [lambda i=i: right[i] for i, j in EARLY],
        buffers, use,
        [functools.partial(upper_halves, 0), functools.partial(upper_halves, 2), last_quarters],
    )


def above_own(
    sent, left, right, above, before, totals, leaving, tiles,
    left_above, right_above, passed, *buffers,
):
    totals[...] = before[...]
    passed[...] = jnp.zeros_like(passed)
    for j in range(4):
        left_rows, right_rows = neighbour_features(above[j, 16:32, :], 1.0)
        left_above[j] = jnp.transpose(left_rows).astype(bf16)
        right_above[j] = right_rows.astype(bf16)

    def use(step, tile):
        tiles[step] = tile
        if step < 16:
            i, j = step % 4, step // 4
            totals[i] += times(above[j, 0:16, :], tile)
            passed[j] += times_transposed(sent[i, 0:16, :], tile)
        else:
            j, border = CROSS[step - 16]
            passed[j] += times(sent[border, 0:16, :], tile)

    sweep(
        [lambda j=step // 4: left_above[j] for step in range(16)]
        + [lambda border=border: left[border] for j, border in CROSS],
        [lambda i=step % 4: right[i] for step in range(16)]
        + [lambda j=j: right_above[j] for j, border in CROSS],
        buffers, use,
    )
    leaving[...] = passed[...].astype(bf16)


def borders(sent, left, right, above, before, totals, tiles, left_above, *buffers):
    totals[...] = before[...]
    for j in range(5):
        left_above[j] = jnp.transpose(
            neighbour_features(above[4 + j, 16:32, :], 1.0)[0]
        ).astype(bf16)

    def use(step, tile):
        if step < len(LATE):
            i, j = LATE[step]
            tiles[step] = tile
            totals[i] += times(sent[j, 0:16, :], tile)
        else:
            i, j = CROSS[step - len(LATE)]
            totals[i] += times(above[j, 0:16, :], tile)

    sweep(
        [lambda j=j: left[j] for i, j in LATE] + [lambda j=j: left_above[j - 4] for i, j in CROSS],
        [lambda i=i: right[i] for i, j in LATE + CROSS],
        buffers, use,
    )


def finish_image(totals, arrived, own_noise, own_sides, image, rounded):
    value = (totals[...] + arrived[...].astype(f32)) * (1.0 / 256.0) + own_noise[...] * own_sides[...]
    image[...] = value
    rounded[...] = value.astype(bf16)


def gram(first, second):
    return lax.dot_general(
        first, second, (((1,), (1,)), ((), ())),
        precision=lax.Precision.HIGHEST, preferred_element_type=f32,
    )


def side_by_side(blocks):
    return jnp.concatenate(blocks, axis=1)


def inside(own_sides, image, rounded, own_noise, tiles, products, partial, for_row):
    for_row[...] = rounded[2:4]
    both = jnp.concatenate(
        [side_by_side([image[i] for i in range(4)]), side_by_side([own_sides[i] for i in range(4)])],
        axis=0,
    )
    products[...] = gram(both, both)
    double = [jnp.zeros((RHS, BLOCK), f32)] * 4
    for step, (i, j) in enumerate(PAIRED):
        double[i] += times(rounded[j], tiles[PACKED + step])
    for i in range(4):
        start = i % 2 * HALF
        upper = times(rounded[i, :, 0:HALF], tiles[i // 2, start:start + HALF, :])
        down = i // 2 * HALF
        last = times(rounded[i, :, HALF:BLOCK], tiles[2, down:down + HALF, start:start + HALF])
        single = jnp.concatenate([upper[:, 0:HALF], 2.0 * upper[:, HALF:BLOCK] + last], axis=1)
        partial[i] = own_noise[i] * image[i] * 256.0 + single + 2.0 * double[i]


def upward(upper, tiles, before, partial):
    double = [jnp.zeros((RHS, BLOCK), f32)] * 4
    for step in range(16):
        double[step % 4] += times(upper[step // 4], tiles[step])
    for i in range(4):
        partial[i] = before[i] + 2.0 * double[i]


def cross_products(border, tiles_early, tiles_late, tiles_up, single, raised):
    first = len(CROSS) - len(LATE)
    for step, (i, j) in enumerate(CROSS):
        if j in border:
            tile = tiles_early[PACKED + 6 + step] if step < first else tiles_late[step - first]
            single[i] += times(border[j], tile)
            raised[i] += times(border[j], tiles_up[16 + step])


def by_row(from_row, from_corner, upper, tiles_early, tiles_late, tiles_up, before, image, third):
    border = {6: from_row[0], 7: from_row[1], 8: from_corner[0]}
    single = [before[i] for i in range(4)]
    raised = [jnp.zeros((RHS, BLOCK), f32)] * 4
    cross_products(border, tiles_early, tiles_late, tiles_up, single, raised)
    third[...] = gram(
        side_by_side([image[i] for i in range(4)] + [upper[i].astype(f32) for i in range(4)]),
        side_by_side(single + [2.0 * raised[i] for i in range(4)]),
    )


def by_column(from_column, upper, tiles_early, tiles_late, tiles_up, so_far, image, products, copies):
    border = {4: from_column[0], 5: from_column[1]}
    single = [jnp.zeros((RHS, BLOCK), f32)] * 4
    raised = [jnp.zeros((RHS, BLOCK), f32)] * 4
    cross_products(border, tiles_early, tiles_late, tiles_up, single, raised)
    third = (so_far[...] + gram(
        side_by_side([image[i] for i in (1, 3)] + [upper[i].astype(f32) for i in (1, 3)]),
        side_by_side([single[i] for i in (1, 3)] + [2.0 * raised[i] for i in (1, 3)]),
    )) * (1.0 / 256.0)
    known = products[...]
    ordered = jnp.concatenate(
        [known[16:32, 16:32], known[16:32, 0:16], known[0:16, 0:16], third], axis=1
    )
    packed = jnp.concatenate([ordered[0:8], ordered[8:16]], axis=1)
    copies[...] = jnp.broadcast_to(packed[None], copies.shape)


def add_up(arrived, copies):
    copies[...] = jnp.broadcast_to(jnp.sum(arrived[...], axis=0, keepdims=True), copies.shape)


def inverse_of_two(block):
    (a, b), (c, d) = block
    scale = 1.0 / (a * d - b * c)
    return ((d * scale, -b * scale), (-c * scale, a * scale))


def product_of_two(first, second):
    return tuple(
        tuple(first[p][0] * second[0][q] + first[p][1] * second[1][q] for q in range(2))
        for p in range(2)
    )


def eliminate_four(value, rows, k):
    columns = [jnp.broadcast_to(value[:, k + q:k + q + 1], value.shape) for q in range(4)]
    lines = [value[k + q:k + q + 1] for q in range(4)]
    pivot = [[columns[q][k + p:k + p + 1] for q in range(4)] for p in range(4)]

    def block(p, q):
        return ((pivot[p][q], pivot[p][q + 1]), (pivot[p + 1][q], pivot[p + 1][q + 1]))

    head = inverse_of_two(block(0, 0))
    right = block(0, 2)
    reduced = product_of_two(block(2, 0), head)
    corner = block(2, 2)
    taken = product_of_two(reduced, right)
    tail = inverse_of_two(
        tuple(tuple(corner[p][q] - taken[p][q] for q in range(2)) for p in range(2))
    )
    low = [lines[2 + p] - (reduced[p][0] * lines[0] + reduced[p][1] * lines[1]) for p in range(2)]
    low = [tail[p][0] * low[0] + tail[p][1] * low[1] for p in range(2)]
    high = [lines[p] - (right[p][0] * low[0] + right[p][1] * low[1]) for p in range(2)]
    high = [head[p][0] * high[0] + head[p][1] * high[1] for p in range(2)]
    new = high + low
    value = (value - columns[0] * new[0] - columns[1] * new[1]) - (
        columns[2] * new[2] + columns[3] * new[3]
    )
    for q in range(4):
        value = jnp.where(rows == k + q, new[q], value)
    return value


def conclude(arrived, own_sides, image, result):
    packed = jnp.sum(arrived[...], axis=0)
    ordered = jnp.concatenate([packed[:, 0:64], packed[:, 64:128]], axis=0)
    start, first, second, third = (ordered[:, 16 * part:16 * part + 16] for part in range(4))
    square = jnp.concatenate(
        [jnp.concatenate([first, second], axis=1), jnp.concatenate([second, third], axis=1)], axis=0
    )
    square = jnp.concatenate([square, jnp.zeros((32, 96), f32)], axis=1)
    flipped = jnp.transpose(jnp.concatenate([square, jnp.zeros((96, 128), f32)], axis=0))[0:32]
    square = 0.5 * (square + flipped)
    known = jnp.concatenate([start, square[0:16, 0:16]], axis=0)
    value = jnp.concatenate([square[:, 0:32], known, jnp.zeros((32, 80), f32)], axis=1)
    rows = lax.broadcasted_iota(jnp.int32, (32, 128), 0)
    for k in range(0, 32, 4):
        value = eliminate_four(value, rows, k)
    weights = jnp.transpose(jnp.concatenate([value, jnp.zeros((96, 128), f32)], axis=0))[32:48, 0:32]
    member = lax.axis_index("sub")
    for i, (row, column) in enumerate(OWN):
        both = jnp.concatenate([own_sides[i], image[i]], axis=0)
        place = (row ^ (member & 1)) + 2 * (column ^ (member >> 1))
        result[place] = jnp.dot(
            weights, both, precision=lax.Precision.HIGHEST, preferred_element_type=f32
        )


def local(regions, members, points, noise_var, right_sides, pair_list, pair_count):
    everyone = regions * members

    def from_region(value, step):
        pairs = [
            (source, source - step)
            for source in range(regions)
            if 0 <= source - step < regions
        ]
        return lax.ppermute(value, "region", pairs)

    def from_member(value, mask):
        return lax.ppermute(value, "sub", [(source, source ^ mask) for source in range(members)])

    def swap(copies, stride):
        size = copies.shape[0]
        groups = [
            [first + stride * place for place in range(size)]
            for first in range(everyone)
            if first // stride % size == 0
        ]
        return lax.all_to_all(
            copies, ("region", "sub"), 0, 0, axis_index_groups=groups, tiled=True
        )

    def shape(*dims, dtype=f32):
        return jax.ShapeDtypeStruct(dims, dtype)

    def held(*dims, dtype=bf16):
        return pltpu.VMEM(dims, dtype)

    tile_flops = 2 * BLOCK * BLOCK * 256
    field = (4, RHS, BLOCK)
    buffers = [pltpu.VMEM((BLOCK, BLOCK), f32)] * 2
    sent, left, right, own_sides, own_noise = call(
        prepare, "prepare",
        (shape(9, 32, BLOCK, dtype=bf16), shape(9, BLOCK, FEATURES, dtype=bf16),
         shape(4, FEATURES, BLOCK, dtype=bf16), shape(*field), shape(4, 1, BLOCK)),
        [pltpu.with_memory_space_constraint(value, pltpu.HBM) for value in (points, noise_var, right_sides)],
        tile_flops,
        [pltpu.VMEM(value.shape, f32) for value in (points, noise_var, right_sides)]
        + [pltpu.SemaphoreType.DMA((3,))],
        pltpu.HBM,
    )
    above = from_region(sent, 1)
    totals, tiles_early = call(
        within_layer, "within_layer", (shape(*field), held(PACKED + len(EARLY), BLOCK, BLOCK)),
        (sent, left, right), (PACKED + len(EARLY)) * 4 * tile_flops, buffers,
    )
    totals, passed, tiles_up = call(
        above_own, "above_own",
        (shape(*field), shape(*field, dtype=bf16), held(25, BLOCK, BLOCK)),
        (sent, left, right, above, totals), 25 * 4 * tile_flops,
        [pltpu.VMEM((4, BLOCK, FEATURES), bf16), pltpu.VMEM((4, FEATURES, BLOCK), bf16),
         pltpu.VMEM(field, f32)] + buffers,
    )
    arrived = from_region(passed, -1)
    totals, tiles_late = call(
        borders, "borders", (shape(*field), held(len(LATE), BLOCK, BLOCK)),
        (sent, left, right, above, totals), 16 * 4 * tile_flops,
        [pltpu.VMEM((5, BLOCK, FEATURES), bf16)] + buffers,
    )
    image, rounded = call(
        finish_image, "finish_image", (shape(*field), shape(*field, dtype=bf16)),
        (totals, arrived, own_noise, own_sides), tile_flops // 8,
    )
    upper = from_region(rounded, 1)
    from_column = from_member(rounded[1::2], 2)
    from_corner = from_member(rounded[3:4], 3)
    products, partial, for_row = call(
        inside, "inside", (shape(32, 32), shape(*field), shape(2, RHS, BLOCK, dtype=bf16)),
        (own_sides, image, rounded, own_noise, tiles_early), 10 * 2 * tile_flops,
    )
    from_row = from_member(for_row, 1)
    partial = call(
        upward, "upward", shape(*field), (upper, tiles_up, partial), 16 * 2 * tile_flops,
    )
    third = call(
        by_row, "by_row", shape(RHS, RHS),
        (from_row, from_corner, upper, tiles_early, tiles_late, tiles_up, partial, image),
        10 * 2 * tile_flops,
    )
    plane = 8 * members
    copies = call(
        by_column, "by_column", shape(plane, 8, 128),
        (from_column, upper, tiles_early, tiles_late, tiles_up, third, image, products),
        8 * 2 * tile_flops,
    )
    arrived = swap(copies, 1)
    copies = call(add_up, "add_up", shape(everyone // plane, 8, 128), (arrived,), 1024)
    arrived = swap(copies, plane)
    return call(
        conclude, "conclude", shape(*field), (arrived, own_sides, image), tile_flops,
    )


def solution(mesh):
    return jax.shard_map(
        functools.partial(local, mesh.shape["region"], mesh.shape["sub"]),
        mesh=mesh,
        in_specs=(
            P(None, "region", None),
            P("region", None),
            P("region", None, None),
            P("region", "sub", None, None),
            P("region", "sub"),
        ),
        out_specs=P(("region", "sub"), None, None),
        check_vma=False,
    )
```

```python
import functools
import jax
import jax.numpy as jnp
from jax import lax
from jax.experimental import pallas as pl
from jax.experimental.pallas import tpu as pltpu
from jax.sharding import PartitionSpec as P

OWN = ((0, 0), (0, 1), (1, 0), (1, 1))
BORDER = ((0, 2), (1, 2), (2, 0), (2, 1), (2, 2))
WINDOW = OWN + BORDER
PAIRED = tuple((i, j) for j in range(4) for i in range(j))
CROSS = tuple(
    (i, j)
    for j in range(4, 9)
    for i in range(4)
    if max(abs(OWN[i][0] - WINDOW[j][0]), abs(OWN[i][1] - WINDOW[j][1])) <= 1
)
HALF = 256
PACKED = 3
EARLY = PAIRED + CROSS[:6]
LATE = CROSS[6:]
BLOCK = 512
RHS = 16
FEATURES = 64
f32, bf16 = jnp.float32, jnp.bfloat16
VMEM = pl.BlockSpec(memory_space=pltpu.VMEM)


def call(kernel, name, out_shape, args, flops, scratch=(), args_space=pltpu.VMEM):
    return pl.pallas_call(
        kernel,
        name=name,
        out_shape=out_shape,
        in_specs=[pl.BlockSpec(memory_space=args_space)] * len(args),
        out_specs=jax.tree.map(lambda _: VMEM, out_shape),
        scratch_shapes=scratch,
        compiler_params=pltpu.CompilerParams(vmem_limit_bytes=16 << 20),
        cost_estimate=pl.CostEstimate(flops=flops, bytes_accessed=1 << 20, transcendentals=0),
    )(*args)


def split(value):
    high = value.astype(bf16).astype(f32)
    rest = value - high
    middle = rest.astype(bf16).astype(f32)
    return high, middle, rest - middle


def feature_rows(place):
    rows = lax.broadcasted_iota(jnp.int32, place.shape, 0)
    parts = split(place)
    norms = split(16.0 * jnp.sum(place * place, axis=0, keepdims=True))
    left, right = [], []
    for group, (a, b) in enumerate(((0, 0), (0, 1), (1, 0), (1, 1), (0, 2), (2, 0), (1, 2), (2, 1))):
        one_left, one_right = -32.0 * parts[a], parts[b]
        if group < 3:
            norm = jnp.broadcast_to(norms[group], place.shape)
            one_left = jnp.where(rows == 3, norm, jnp.where(rows == 4, 1.0, one_left))
            one_right = jnp.where(rows == 4, norm, jnp.where(rows == 3, 1.0, one_right))
        left.append(one_left)
        right.append(one_right)
    return jnp.concatenate(left, axis=0), jnp.concatenate(right, axis=0)


def prepare(
    points_far, noise_far, sides_far, sent, left, right, own_sides, own_noise,
    points, noise_var, right_sides, arrivals,
):
    copies = [
        pltpu.make_async_copy(source, target, arrivals.at[place])
        for place, (source, target) in enumerate(
            ((points_far, points), (noise_far, noise_var), (sides_far, right_sides))
        )
    ]
    for copy in copies:
        copy.start()
    copies[0].wait()
    region = lax.axis_index("region")
    member = lax.axis_index("sub")
    row_half, column_half = member & 1, member >> 1
    rows = lax.broadcasted_iota(jnp.int32, (8, BLOCK), 0)
    centers = (
        region.astype(f32) + 0.5,
        row_half.astype(f32) + 1.5,
        column_half.astype(f32) + 1.5,
    )
    blocks = []
    for index, (row, column) in enumerate(WINDOW):
        row = jnp.where(row_half == 1, 3 - row, row)
        column = jnp.where(column_half == 1, 3 - column, column)
        block = (row & 1) + 2 * (column & 1) + 4 * (row >> 1) + 8 * (column >> 1)
        place = jnp.zeros((8, BLOCK), f32)
        for axis in range(3):
            line = points[axis, pl.ds(block, 1), :] - centers[axis]
            place = jnp.where(rows == axis, jnp.broadcast_to(line, place.shape), place)
        blocks.append(block)
        high, middle, low = split(place)
        sent[index, 16:32, :] = jnp.concatenate(
            [high + pltpu.roll(low, 3, 0), middle], axis=0
        ).astype(bf16)
        left_rows, right_rows = feature_rows(place)
        left[index] = jnp.transpose(left_rows).astype(bf16)
        if index < 4:
            right[index] = right_rows.astype(bf16)
    copies[1].wait()
    copies[2].wait()
    for index, block in enumerate(blocks):
        side = right_sides[block]
        sent[index, 0:16, :] = side.astype(bf16)
        if index < 4:
            own_sides[index] = side
            own_noise[index] = noise_var[pl.ds(block, 1), :]


def neighbour_features(packed, shift):
    rows = lax.broadcasted_iota(jnp.int32, (8, BLOCK), 0)
    packed = packed.astype(f32)
    top, middle = packed[0:8], packed[8:16]
    place = jnp.where(rows < 3, top + middle + pltpu.roll(top, 5, 0), 0.0)
    place = jnp.where(rows == 0, place + shift, place)
    return feature_rows(place)


def sweep(lefts, rights, buffers, use, fills=()):
    count = len(fills) + len(lefts)

    def distances(step):
        buffer = buffers[step % 2]
        if step < len(fills):
            fills[step](buffer)
        else:
            place = step - len(fills)
            buffer[...] = jnp.dot(lefts[place](), rights[place](), preferred_element_type=f32)

    distances(0)
    for step in range(count):
        if step + 1 < count:
            distances(step + 1)
        parts = []
        for start in range(0, BLOCK, 64):
            squared = jnp.maximum(buffers[step % 2][start:start + 64, :], 1e-30)
            falloff = jnp.maximum(4.0 - squared * lax.rsqrt(squared), 0.0)
            second = falloff * falloff
            parts.append(((second * second) * (5.0 - falloff)).astype(bf16))
        use(step, jnp.concatenate(parts, axis=0))


def times(vectors, tile):
    return jnp.dot(vectors, tile, preferred_element_type=f32)


def times_transposed(vectors, tile):
    return lax.dot_general(vectors, tile, (((1,), (1,)), ((), ())), preferred_element_type=f32)


def within_layer(sent, left, right, totals, tiles, *buffers):
    totals[...] = jnp.zeros_like(totals)

    def upper_halves(first, buffer):
        for place in range(2):
            i = first + place
            buffer[place * HALF:(place + 1) * HALF, :] = jnp.dot(
                left[i, 0:HALF, :], right[i], preferred_element_type=f32
            )

    def last_quarters(buffer):
        for i in range(4):
            down, along = i // 2 * HALF, i % 2 * HALF
            buffer[down:down + HALF, along:along + HALF] = jnp.dot(
                left[i, HALF:BLOCK, :], right[i, :, HALF:BLOCK], preferred_element_type=f32
            )

    def use(step, tile):
        tiles[step] = tile
        if step < 2:
            for place in range(2):
                i = 2 * step + place
                part = tile[place * HALF:(place + 1) * HALF, :]
                totals[i] += times(sent[i, 0:16, 0:HALF], part)
                totals[i, :, 0:HALF] += times_transposed(sent[i, 0:16, HALF:BLOCK], part[:, HALF:BLOCK])
        elif step == 2:
            for i in range(4):
                down, along = i // 2 * HALF, i % 2 * HALF
                part = tile[down:down + HALF, along:along + HALF]
                totals[i, :, HALF:BLOCK] += times(sent[i, 0:16, HALF:BLOCK], part)
        else:
            i, j = EARLY[step - PACKED]
            totals[i] += times(sent[j, 0:16, :], tile)
            if j < 4:
                totals[j] += times_transposed(sent[i, 0:16, :], tile)

    sweep(
        [lambda j=j: left[j] for i, j in EARLY],
        [lambda i=i: right[i] for i, j in EARLY],
        buffers, use,
        [functools.partial(upper_halves, 0), functools.partial(upper_halves, 2), last_quarters],
    )


def above_own(
    sent, left, right, above, before, totals, leaving, tiles,
    left_above, right_above, passed, *buffers,
):
    totals[...] = before[...]
    passed[...] = jnp.zeros_like(passed)
    for j in range(4):
        left_rows, right_rows = neighbour_features(above[j, 16:32, :], 1.0)
        left_above[j] = jnp.transpose(left_rows).astype(bf16)
        right_above[j] = right_rows.astype(bf16)

    def use(step, tile):
        tiles[step] = tile
        if step < 16:
            i, j = step % 4, step // 4
            totals[i] += times(above[j, 0:16, :], tile)
            passed[j] += times_transposed(sent[i, 0:16, :], tile)
        else:
            j, border = CROSS[step - 16]
            passed[j] += times(sent[border, 0:16, :], tile)

    sweep(
        [lambda j=step // 4: left_above[j] for step in range(16)]
        + [lambda border=border: left[border] for j, border in CROSS],
        [lambda i=step % 4: right[i] for step in range(16)]
        + [lambda j=j: right_above[j] for j, border in CROSS],
        buffers, use,
    )
    leaving[...] = passed[...].astype(bf16)


def borders(sent, left, right, above, before, totals, tiles, left_above, *buffers):
    totals[...] = before[...]
    for j in range(5):
        left_above[j] = jnp.transpose(
            neighbour_features(above[4 + j, 16:32, :], 1.0)[0]
        ).astype(bf16)

    def use(step, tile):
        if step < len(LATE):
            i, j = LATE[step]
            tiles[step] = tile
            totals[i] += times(sent[j, 0:16, :], tile)
        else:
            i, j = CROSS[step - len(LATE)]
            totals[i] += times(above[j, 0:16, :], tile)

    sweep(
        [lambda j=j: left[j] for i, j in LATE] + [lambda j=j: left_above[j - 4] for i, j in CROSS],
        [lambda i=i: right[i] for i, j in LATE + CROSS],
        buffers, use,
    )


def finish_image(totals, arrived, own_noise, own_sides, image, rounded):
    value = (totals[...] + arrived[...].astype(f32)) * (1.0 / 256.0) + own_noise[...] * own_sides[...]
    image[...] = value
    rounded[...] = value.astype(bf16)


def gram(first, second):
    return lax.dot_general(
        first, second, (((1,), (1,)), ((), ())),
        precision=lax.Precision.HIGHEST, preferred_element_type=f32,
    )


def side_by_side(blocks):
    return jnp.concatenate(blocks, axis=1)


def inside(own_sides, image, rounded, own_noise, tiles, products, partial):
    both = jnp.concatenate(
        [side_by_side([image[i] for i in range(4)]), side_by_side([own_sides[i] for i in range(4)])],
        axis=0,
    )
    products[...] = gram(both, both)
    double = [jnp.zeros((RHS, BLOCK), f32)] * 4
    for step, (i, j) in enumerate(PAIRED):
        double[i] += times(rounded[j], tiles[PACKED + step])
    for i in range(4):
        start = i % 2 * HALF
        upper = times(rounded[i, :, 0:HALF], tiles[i // 2, start:start + HALF, :])
        down = i // 2 * HALF
        last = times(rounded[i, :, HALF:BLOCK], tiles[2, down:down + HALF, start:start + HALF])
        single = jnp.concatenate([upper[:, 0:HALF], 2.0 * upper[:, HALF:BLOCK] + last], axis=1)
        partial[i] = own_noise[i] * image[i] * 256.0 + single + 2.0 * double[i]


def upward(upper, tiles, before, image, third):
    double = [jnp.zeros((RHS, BLOCK), f32)] * 4
    for step in range(16):
        double[step % 4] += times(upper[step // 4], tiles[step])
    third[...] = gram(
        side_by_side([image[i] for i in range(4)]),
        side_by_side([before[i] + 2.0 * double[i] for i in range(4)]),
    )


def cross_products(border, tiles_early, tiles_late, tiles_up, single, raised):
    first = len(CROSS) - len(LATE)
    for step, (i, j) in enumerate(CROSS):
        if j in border:
            tile = tiles_early[PACKED + 6 + step] if step < first else tiles_late[step - first]
            single[i] += times(border[j], tile)
            raised[i] += times(border[j], tiles_up[16 + step])


def by_column(from_column, so_far, tiles_early, tiles_late, tiles_up, single_out, raised_out):
    border = {4: from_column[0], 5: from_column[1]}
    single = [jnp.zeros((RHS, BLOCK), f32)] * 4
    raised = [jnp.zeros((RHS, BLOCK), f32)] * 4
    cross_products(border, tiles_early, tiles_late, tiles_up, single, raised)
    for i in range(4):
        single_out[i] = single[i]
        raised_out[i] = raised[i]


def by_row(
    from_row, from_corner, upper, tiles_early, tiles_late, tiles_up, single_in, raised_in,
    so_far, image, products, copies,
):
    border = {6: from_row[0], 7: from_row[1], 8: from_corner[0]}
    single = [single_in[i] for i in range(4)]
    raised = [raised_in[i] for i in range(4)]
    cross_products(border, tiles_early, tiles_late, tiles_up, single, raised)
    third = (so_far[...] + gram(
        side_by_side([image[i] for i in range(1, 4)] + [upper[i].astype(f32) for i in range(1, 4)]),
        side_by_side([single[i] for i in range(1, 4)] + [2.0 * raised[i] for i in range(1, 4)]),
    )) * (1.0 / 256.0)
    known = products[...]
    ordered = jnp.concatenate(
        [known[16:32, 16:32], known[16:32, 0:16], known[0:16, 0:16], third], axis=1
    )
    packed = jnp.concatenate([ordered[0:8], ordered[8:16]], axis=1)
    copies[...] = jnp.broadcast_to(packed[None], copies.shape)


def add_up(arrived, copies):
    copies[...] = jnp.broadcast_to(jnp.sum(arrived[...], axis=0, keepdims=True), copies.shape)


def inverse_of_two(block):
    (a, b), (c, d) = block
    scale = 1.0 / (a * d - b * c)
    return ((d * scale, -b * scale), (-c * scale, a * scale))


def product_of_two(first, second):
    return tuple(
        tuple(first[p][0] * second[0][q] + first[p][1] * second[1][q] for q in range(2))
        for p in range(2)
    )


def eliminate_four(value, rows, k):
    columns = [jnp.broadcast_to(value[:, k + q:k + q + 1], value.shape) for q in range(4)]
    lines = [value[k + q:k + q + 1] for q in range(4)]
    pivot = [[columns[q][k + p:k + p + 1] for q in range(4)] for p in range(4)]

    def block(p, q):
        return ((pivot[p][q], pivot[p][q + 1]), (pivot[p + 1][q], pivot[p + 1][q + 1]))

    head = inverse_of_two(block(0, 0))
    right = block(0, 2)
    reduced = product_of_two(block(2, 0), head)
    corner = block(2, 2)
    taken = product_of_two(reduced, right)
    tail = inverse_of_two(
        tuple(tuple(corner[p][q] - taken[p][q] for q in range(2)) for p in range(2))
    )
    low = [lines[2 + p] - (reduced[p][0] * lines[0] + reduced[p][1] * lines[1]) for p in range(2)]
    low = [tail[p][0] * low[0] + tail[p][1] * low[1] for p in range(2)]
    high = [lines[p] - (right[p][0] * low[0] + right[p][1] * low[1]) for p in range(2)]
    high = [head[p][0] * high[0] + head[p][1] * high[1] for p in range(2)]
    new = high + low
    value = (value - columns[0] * new[0] - columns[1] * new[1]) - (
        columns[2] * new[2] + columns[3] * new[3]
    )
    for q in range(4):
        value = jnp.where(rows == k + q, new[q], value)
    return value


def conclude(arrived, own_sides, image, result):
    packed = jnp.sum(arrived[...], axis=0)
    ordered = jnp.concatenate([packed[:, 0:64], packed[:, 64:128]], axis=0)
    start, first, second, third = (ordered[:, 16 * part:16 * part + 16] for part in range(4))
    square = jnp.concatenate(
        [jnp.concatenate([first, second], axis=1), jnp.concatenate([second, third], axis=1)], axis=0
    )
    square = jnp.concatenate([square, jnp.zeros((32, 96), f32)], axis=1)
    flipped = jnp.transpose(jnp.concatenate([square, jnp.zeros((96, 128), f32)], axis=0))[0:32]
    square = 0.5 * (square + flipped)
    known = jnp.concatenate([start, square[0:16, 0:16]], axis=0)
    value = jnp.concatenate([square[:, 0:32], known, jnp.zeros((32, 80), f32)], axis=1)
    rows = lax.broadcasted_iota(jnp.int32, (32, 128), 0)
    for k in range(0, 32, 4):
        value = eliminate_four(value, rows, k)
    weights = jnp.transpose(jnp.concatenate([value, jnp.zeros((96, 128), f32)], axis=0))[32:48, 0:32]
    member = lax.axis_index("sub")
    for i, (row, column) in enumerate(OWN):
        both = jnp.concatenate([own_sides[i], image[i]], axis=0)
        place = (row ^ (member & 1)) + 2 * (column ^ (member >> 1))
        result[place] = jnp.dot(
            weights, both, precision=lax.Precision.HIGHEST, preferred_element_type=f32
        )


def local(regions, members, points, noise_var, right_sides, pair_list, pair_count):
    everyone = regions * members

    def from_region(value, step):
        pairs = [
            (source, source - step)
            for source in range(regions)
            if 0 <= source - step < regions
        ]
        return lax.ppermute(value, "region", pairs)

    def from_member(value, mask):
        return lax.ppermute(value, "sub", [(source, source ^ mask) for source in range(members)])

    def swap(copies, stride):
        size = copies.shape[0]
        groups = [
            [first + stride * place for place in range(size)]
            for first in range(everyone)
            if first // stride % size == 0
        ]
        return lax.all_to_all(
            copies, ("region", "sub"), 0, 0, axis_index_groups=groups, tiled=True
        )

    def shape(*dims, dtype=f32):
        return jax.ShapeDtypeStruct(dims, dtype)

    def held(*dims, dtype=bf16):
        return pltpu.VMEM(dims, dtype)

    tile_flops = 2 * BLOCK * BLOCK * 256
    field = (4, RHS, BLOCK)
    buffers = [pltpu.VMEM((BLOCK, BLOCK), f32)] * 2
    sent, left, right, own_sides, own_noise = call(
        prepare, "prepare",
        (shape(9, 32, BLOCK, dtype=bf16), shape(9, BLOCK, FEATURES, dtype=bf16),
         shape(4, FEATURES, BLOCK, dtype=bf16), shape(*field), shape(4, 1, BLOCK)),
        [pltpu.with_memory_space_constraint(value, pltpu.HBM) for value in (points, noise_var, right_sides)],
        tile_flops,
        [pltpu.VMEM(value.shape, f32) for value in (points, noise_var, right_sides)]
        + [pltpu.SemaphoreType.DMA((3,))],
        pltpu.HBM,
    )
    above = from_region(sent, 1)
    totals, tiles_early = call(
        within_layer, "within_layer", (shape(*field), held(PACKED + len(EARLY), BLOCK, BLOCK)),
        (sent, left, right), (PACKED + len(EARLY)) * 4 * tile_flops, buffers,
    )
    totals, passed, tiles_up = call(
        above_own, "above_own",
        (shape(*field), shape(*field, dtype=bf16), held(25, BLOCK, BLOCK)),
        (sent, left, right, above, totals), 25 * 4 * tile_flops,
        [pltpu.VMEM((4, BLOCK, FEATURES), bf16), pltpu.VMEM((4, FEATURES, BLOCK), bf16),
         pltpu.VMEM(field, f32)] + buffers,
    )
    arrived = from_region(passed, -1)
    totals, tiles_late = call(
        borders, "borders", (shape(*field), held(len(LATE), BLOCK, BLOCK)),
        (sent, left, right, above, totals), 16 * 4 * tile_flops,
        [pltpu.VMEM((5, BLOCK, FEATURES), bf16)] + buffers,
    )
    image, rounded = call(
        finish_image, "finish_image", (shape(*field), shape(*field, dtype=bf16)),
        (totals, arrived, own_noise, own_sides), tile_flops // 8,
    )
    upper = from_region(rounded, 1)
    from_row = from_member(rounded[2:4], 1)
    from_column = from_member(rounded[1::2], 2)
    from_corner = from_member(rounded[3:4], 3)
    products, partial = call(
        inside, "inside", (shape(32, 32), shape(*field)),
        (own_sides, image, rounded, own_noise, tiles_early), 10 * 2 * tile_flops,
    )
    third = call(
        upward, "upward", shape(RHS, RHS), (upper, tiles_up, partial, image), 16 * 2 * tile_flops,
    )
    single, raised = call(
        by_column, "by_column", (shape(*field), shape(*field)),
        (from_column, third, tiles_early, tiles_late, tiles_up), 8 * 2 * tile_flops,
    )
    plane = 8 * members
    copies = call(
        by_row, "by_row", shape(plane, 8, 128),
        (from_row, from_corner, upper, tiles_early, tiles_late, tiles_up, single, raised,
         third, image, products),
        10 * 2 * tile_flops,
    )
    arrived = swap(copies, 1)
    copies = call(add_up, "add_up", shape(everyone // plane, 8, 128), (arrived,), 1024)
    arrived = swap(copies, plane)
    return call(
        conclude, "conclude", shape(*field), (arrived, own_sides, image), tile_flops,
    )


def solution(mesh):
    return jax.shard_map(
        functools.partial(local, mesh.shape["region"], mesh.shape["sub"]),
        mesh=mesh,
        in_specs=(
            P(None, "region", None),
            P("region", None),
            P("region", None, None),
            P("region", "sub", None, None),
            P("region", "sub"),
        ),
        out_specs=P(("region", "sub"), None, None),
        check_vma=False,
    )
```
